256 devices in a mesh: ctx: 64 (over z, y, core), head: 4 (over x).
Axes of the slice: x: 4, y: 4, z: 8, core: 2. Of those that a mesh axis runs over, the one named last changes fastest.
Arguments:
- queries: bfloat16 [24576, 2048], P('ctx', 'head'), may hold values from -8 to 8
- keys: bfloat16 [24576, 512], P('ctx', 'head'), may hold values from -8 to 8
- values: bfloat16 [24576, 512], P('ctx', 'head'), may hold values from -25 to 25
- weight_q: bfloat16 [16, 128, 64], P('head'), may hold values from -0.5 to 0.5
- weight_k: bfloat16 [4, 128, 64], P('head'), may hold values from -0.5 to 0.5
Outputs:
- teacher: bfloat16 [24576, 2048], P('ctx', 'head')
- loss: float32 [], replicated
- grad_q: float32 [16, 128, 64], P('head')
- grad_k: float32 [4, 128, 64], P('head')
The draws below stay inside these ranges and needn't reach their ends.
All inputs are finite; a program needn't handle non-finite values.
Results may differ from the reference program's by a relative error of at most 0.012.
Values may be sent and summed in bfloat16 or wider, within the bound.
No kernel may reach another device: no remote copies, remote signals or barrier semaphores. Data moves between devices by JAX's collectives and lax.ppermute only.
A program may use at most 64 MiB of HBM per device.

```python
import math
import jax
import jax.numpy as jnp
from jax import lax

HD = 128
FD = 64
KVH = 4
GROUP = 4
QH = 16
TOK_DEV = 384
TOKENS = 24576


def draw_queries(key, part):
    key = jax.random.fold_in(key, 11)
    base = jax.random.truncated_normal(key, -3.2, 3.2, (TOKENS, QH * HD), jnp.float32) * 2.5
    return base.astype(jnp.bfloat16)


def draw_keys(key, part):
    key = jax.random.fold_in(key, 12)
    base = jax.random.truncated_normal(key, -4.0, 4.0, (TOKENS, KVH * HD), jnp.float32)
    return base.astype(jnp.bfloat16)


def draw_values(key, part):
    key = jax.random.fold_in(key, 13)
    parts = jax.random.split(key, 5)
    row_scale = jnp.exp(jax.random.uniform(parts[1], (TOKENS, 1), jnp.float32, math.log(0.5), math.log(2.5)))
    col_scale = jnp.exp(jax.random.uniform(parts[2], (1, KVH * HD), jnp.float32, math.log(0.5), math.log(2.5)))
    blocks = TOKENS // TOK_DEV
    magnitude = jax.random.uniform(parts[3], (blocks, 1, KVH * HD), jnp.float32, 1.0, 2.0)
    signs = (jax.random.randint(parts[4], (blocks, 1, KVH * HD), 0, 2) * 2 - 1).astype(jnp.float32)
    offset = jnp.broadcast_to(magnitude * signs, (blocks, TOK_DEV, KVH * HD)).reshape(TOKENS, KVH * HD)
    base = jax.random.truncated_normal(parts[0], -3.2, 3.2, (TOKENS, KVH * HD), jnp.float32)
    base = base * row_scale
    return ((base + offset) * col_scale).astype(jnp.bfloat16)


def level_of(own_key, shape, cuts, smallest, top_value):
    def one(axis_at, shards_of):
        draws = jax.random.uniform(jax.random.fold_in(jax.random.fold_in(own_key, 6), axis_at), (shards_of,), jnp.float32, smallest / len(cuts), top_value / len(cuts))
        return jnp.repeat(jnp.exp(draws), shape[axis_at] // shards_of).reshape((-1,) + (1,) * (len(shape) - axis_at - 1))

    factor_of = one(*cuts[0])
    for cut in cuts[1:]:
        factor_of = factor_of * one(*cut)
    return factor_of


def bell_draw(key, shape, spread, bound, cuts=(), kind=jnp.bfloat16):
    entries = spread * jax.random.normal(key, shape, jnp.float32)
    if cuts:
        entries = entries * level_of(key, shape, cuts, -0.22, 0.18)
    return jnp.clip(entries, -bound, bound).astype(kind)


def setup_inputs(seed: int = 0) -> dict:
    streams_of = jax.random.split(jax.random.key(seed), 6)
    return {
        "queries": draw_queries(jax.random.fold_in(streams_of[5], 71), 0),
        "keys": draw_keys(jax.random.fold_in(streams_of[5], 71), 0),
        "values": draw_values(jax.random.fold_in(streams_of[5], 71), 0),
        "weight_q": bell_draw(streams_of[3], (QH, HD, FD), HD ** -0.5, 0.5, ((0, 4),)),
        "weight_k": bell_draw(streams_of[4], (KVH, HD, FD), HD ** -0.5, 0.5, ((0, 4),)),
    }


HIGHEST = lax.Precision.HIGHEST
NEGATIVE = -1e+30

def features(inputs, weight):
    raised = jnp.einsum('nhd,hdf->nhf', inputs, weight, precision=HIGHEST)
    upper = jnp.exp(raised)
    lower = jnp.exp(-raised)
    upper = upper / lax.optimization_barrier(jnp.sum(upper, -1, keepdims=True))
    lower = lower / lax.optimization_barrier(jnp.sum(lower, -1, keepdims=True))
    return jnp.concatenate([upper, lower], -1)

def teacher_attention(queries, keys, values):
    block = min(512, TOKENS)
    blocks = TOKENS // block
    scale = 1.0 / math.sqrt(HD)
    query_blocks = queries.reshape(blocks, block, KVH, GROUP, HD)
    key_blocks = keys.reshape(blocks, block, KVH, HD)
    value_blocks = values.reshape(blocks, block, KVH, HD)

    def one_block(index):
        query_rows = lax.dynamic_index_in_dim(query_blocks, index, 0, False).astype(jnp.float32)
        row_pos = index * block + jnp.arange(block, dtype=jnp.int32)

        def visit(other, carry):
            best, total, accum = carry
            key_rows = lax.dynamic_index_in_dim(key_blocks, other, 0, False).astype(jnp.float32)
            value_rows = lax.dynamic_index_in_dim(value_blocks, other, 0, False)
            col_pos = other * block + jnp.arange(block, dtype=jnp.int32)
            allowed = col_pos[None, :] <= row_pos[:, None]
            scores = jnp.einsum('nkgd,rkd->kgnr', query_rows, key_rows, precision=HIGHEST) * scale
            scores = jnp.where(allowed, scores, NEGATIVE)
            fresh = jnp.maximum(best, lax.optimization_barrier(jnp.max(scores, -1)))
            weights = jnp.where(allowed, jnp.exp(scores - fresh[..., None]), 0.0)
            fade = jnp.exp(best - fresh)
            total = total * fade + lax.optimization_barrier(jnp.sum(weights, -1))
            rounded = lax.optimization_barrier(weights.astype(jnp.bfloat16)).astype(jnp.float32)
            accum = accum * fade[..., None] + jnp.einsum('kgnr,rkd->kgnd', rounded, value_rows.astype(jnp.float32), precision=HIGHEST)
            return (fresh, total, accum)
        start = (jnp.full((KVH, GROUP, block), NEGATIVE, jnp.float32), jnp.zeros((KVH, GROUP, block), jnp.float32), jnp.zeros((KVH, GROUP, block, HD), jnp.float32))
        best, total, accum = lax.fori_loop(0, index + 1, visit, start)
        output = accum / total[..., None]
        return output.transpose(2, 0, 1, 3).reshape(block, QH * HD).astype(jnp.bfloat16)
    result = lax.map(one_block, jnp.arange(blocks, dtype=jnp.int32))
    return result.reshape(TOKENS, QH * HD)

def student_loss(weight_q, weight_k, queries, keys, values, target):
    block = min(512, TOKENS)
    blocks = TOKENS // block
    feat = 2 * FD
    query_blocks = queries.reshape(blocks, block, QH, HD)
    key_blocks = keys.reshape(blocks, block, KVH, HD)
    value_blocks = values.reshape(blocks, block, KVH, HD)
    target_blocks = target.reshape(blocks, block, KVH, GROUP, HD)
    causal = jnp.tril(jnp.ones((block, block), jnp.float32))

    def step(carry, pieces):
        state, norm, total = carry
        query_rows, key_rows, value_rows, target_rows = pieces
        phi_q = features(query_rows.astype(jnp.float32), weight_q).reshape(block, KVH, GROUP, feat)
        phi_k = features(key_rows.astype(jnp.float32), weight_k)
        value_f = value_rows.astype(jnp.float32)
        scores = jnp.einsum('nkgf,rkf->kgnr', phi_q, phi_k, precision=HIGHEST) * causal
        numer = jnp.einsum('kgnr,rkd->nkgd', scores, value_f, precision=HIGHEST) + jnp.einsum('nkgf,kfd->nkgd', phi_q, state, precision=HIGHEST)
        denom = lax.optimization_barrier(jnp.sum(scores, -1)).transpose(2, 0, 1) + jnp.einsum('nkgf,kf->nkg', phi_q, norm, precision=HIGHEST)
        errors = numer / denom[..., None] - target_rows.astype(jnp.float32)
        total = total + jnp.sum(errors * errors)
        state = state + jnp.einsum('rkf,rkd->kfd', phi_k, value_f, precision=HIGHEST)
        norm = norm + lax.optimization_barrier(jnp.sum(phi_k, 0))
        return ((state, norm, total), None)
    start = (jnp.zeros((KVH, feat, HD), jnp.float32), jnp.zeros((KVH, feat), jnp.float32), jnp.zeros((), jnp.float32))
    (state, norm, total), unused = lax.scan(step, start, (query_blocks, key_blocks, value_blocks, target_blocks))
    return total / (TOKENS * QH)

def reference(queries, keys, values, weight_q, weight_k):
    teacher = teacher_attention(queries, keys, values)

    def objective(first, second):
        return student_loss(first, second, queries, keys, values, teacher)
    loss, pull = jax.vjp(objective, weight_q.astype(jnp.float32), weight_k.astype(jnp.float32))
    grad_q, grad_k = pull(jnp.ones((), jnp.float32))
    return (teacher, loss, grad_q, grad_k)
```

```python
import functools
import math

import jax
import jax.numpy as jnp
from jax import lax
from jax.experimental import pallas as pl
from jax.experimental.pallas import tpu as pltpu
from jax.sharding import Mesh, PartitionSpec as P

F32 = jnp.float32
BF16 = jnp.bfloat16
NEGATIVE = -1e30
TOO_LARGE = 2.0 ** 100
LANES = 128
EXTRA = 8
PAD = 16
NZ, NY, NCORE = 8, 4, 2


def dot(a, b, ca, cb):
    return lax.dot_general(a, b, (((ca,), (cb,)), ((), ())), preferred_element_type=F32)


def split(x):
    high = x.astype(BF16)
    return high, (x - high.astype(F32)).astype(BF16)


def dot_exact_right(x, e, cx, ce):
    high, low = split(x)
    return dot(high, e, cx, ce) + dot(low, e, cx, ce)


def dot_exact_left(e, x, ce, cx):
    high, low = split(x)
    return dot(e, high, ce, cx) + dot(e, low, ce, cx)


def dot_wide(x, y, cx, cy):
    xh, xl = split(x)
    yh, yl = split(y)
    return dot(xh, yh, cx, cy) + (dot(xh, yl, cx, cy) + dot(xl, yh, cx, cy))


def side_by_side(x):
    return jnp.concatenate(split(x), 1)


def halves_added(x):
    half = x.shape[1] // 2
    return x[:, :half] + x[:, half:]


def rows_exact(e, x):
    return halves_added(dot(e, side_by_side(x), 0, 0))


def rows_wide(x, y):
    both = halves_added(dot(side_by_side(x), side_by_side(y), 0, 0))
    half = both.shape[0] // 2
    return both[:half] + both[half:]


def lane_ids(shape):
    return lax.broadcasted_iota(jnp.int32, shape, 1)


def feature_map(x, w2):
    e = jnp.exp(dot(x, w2, 1, 1))
    first = lane_ids(e.shape) < LANES // 2
    upper = jnp.sum(jnp.where(first, e, 0.0), 1, keepdims=True)
    lower = jnp.sum(jnp.where(first, 0.0, e), 1, keepdims=True)
    return e / jnp.where(first, upper, lower)


def signed(w):
    return jnp.concatenate([w, -w], 0)


def feature_pull(phi, grad):
    rows = lax.broadcasted_iota(jnp.int32, (LANES, LANES), 0) < LANES // 2
    cols = lane_ids((LANES, LANES)) < LANES // 2
    ones = jnp.where(rows == cols, 1.0, 0.0).astype(BF16)
    return phi * (grad - dot_exact_right(phi * grad, ones, 1, 0))


def lane_fold(x):
    total = x[:, :LANES]
    for at in range(LANES, x.shape[1], LANES):
        total = total + x[:, at:at + LANES]
    return total


def lane_wide(x, width):
    return jnp.concatenate([x] * (width // LANES), 1)


def lane_at(x, lane):
    return jnp.sum(jnp.where(lane_ids(x.shape) == lane, x, 0.0), 1, keepdims=True)


def lower_triangle(count):
    rows = lax.broadcasted_iota(jnp.int32, (count, count), 0)
    return lane_ids((count, count)) <= rows


def only_row(row, count):
    at = lax.broadcasted_iota(jnp.int32, (count, LANES), 0)
    return jnp.where(at == 0, row, 0.0)


def loop(count, body):
    def visit(index, unused):
        body(index)
        return unused

    lax.fori_loop(0, count, visit, 0)


def add_state(k, v, w2, state_ref):
    phi = feature_map(k, w2)
    state_ref[:LANES, :] += rows_exact(v, phi)
    state_ref[LANES:, :] += only_row(jnp.sum(phi, 0, keepdims=True), PAD)
    return phi


def near_kernel(heads, unit, qk_ref, twin_ref, kv_ref, wq_ref, wk_ref, qs_ref,
                m_ref, l_ref, acc_ref, phik_ref, state_ref, numer_ref, denom_ref):
    count = kv_ref.shape[0]
    v = kv_ref[:, LANES:]
    state_ref[...] = jnp.zeros_like(state_ref)
    denom_ref[...] = jnp.zeros_like(denom_ref)
    phik_ref[...] = add_state(kv_ref[:, :LANES], v, signed(wk_ref[0]), state_ref)
    for h in range(heads):
        qs_ref[h] = qk_ref[:, h * LANES:(h + 1) * LANES]
        qs_ref[heads + h] = twin_ref[:, h * LANES:(h + 1) * LANES]

    def head(h):
        allowed = lower_triangle(count)
        q = qs_ref[h]
        s = jnp.where(allowed, dot(q, kv_ref[:, :LANES], 1, 1) * unit, NEGATIVE)
        best = jnp.max(s, 1, keepdims=True)
        p = jnp.exp2(s - best)
        m_ref[h] = jnp.broadcast_to(best, (count, LANES))
        l_ref[h] = lane_fold(p)
        acc_ref[h] = dot(p.astype(BF16), v, 1, 0)
        twin_k = twin_ref[:, heads * LANES:]
        s = jnp.where(allowed, dot(qs_ref[heads + h], twin_k, 1, 1) * unit, NEGATIVE)
        m_ref[heads + h] = jnp.broadcast_to(jnp.max(s, 1, keepdims=True), (count, LANES))
        l_ref[heads + h] = jnp.zeros((count, LANES), F32)
        acc_ref[heads + h] = jnp.zeros((count, LANES), F32)
        phi = feature_map(q, signed(wq_ref[h]))
        scores = jnp.where(allowed, dot_wide(phi, phik_ref[...], 1, 1), 0.0)
        numer_ref[h] = dot_exact_right(scores, v, 1, 0)
        denom_ref[...] = jnp.where(
            lane_ids((count, LANES)) == h, jnp.sum(scores, 1, keepdims=True), denom_ref[...]
        )

    loop(heads, head)

    def twin_head(h):
        at = heads + h
        s = dot(qs_ref[at], kv_ref[:, :LANES], 1, 1) * unit
        new = jnp.maximum(m_ref[at], jnp.max(s, 1, keepdims=True))
        p = jnp.exp2(s - lane_wide(new, count))
        m_ref[at] = new
        l_ref[at] = lane_fold(p)
        acc_ref[at] = dot(p.astype(BF16), v, 1, 0)

    loop(jnp.where(lax.axis_index("core") == 0, heads, 0), twin_head)


def far_kernel(heads, unit, wanted, last, qs_ref, w_ref, mi_ref, li_ref, ai_ref, si_ref, *refs):
    parts = len(wanted)
    kv_refs, refs = refs[:parts], refs[parts:]
    if last:
        near_ref, mine_ref, twin_ref, m_ref, l_ref, acc_ref, state_ref = refs
    else:
        m_ref, l_ref, acc_ref, state_ref = refs
    counts = [want() for want in wanted]
    tiles, count, _ = qs_ref.shape
    groups = tiles // heads
    keys = kv_refs[0].shape[1]
    m_ref[...] = mi_ref[...]
    l_ref[...] = li_ref[...]
    acc_ref[...] = ai_ref[...]
    state_ref[...] = si_ref[...]

    for at in range(parts):
        kv = kv_refs[at]

        def visit(index, kv=kv):
            j, first = index // groups, lax.rem(index, groups) * heads
            k = kv[j, :, :LANES]
            v = kv[j, :, LANES:]
            following = dot(qs_ref[first], k, 1, 1)
            for h in range(heads):
                t = first + h
                s = following
                if h + 1 < heads:
                    following = dot(qs_ref[t + 1], k, 1, 1)
                p = jnp.exp2(s * unit - lane_wide(m_ref[t], keys))
                l_ref[t] += lane_fold(p)
                acc_ref[t] += dot(p.astype(BF16), v, 1, 0)

        def keep(j, kv=kv):
            add_state(kv[j, :, :LANES], kv[j, :, LANES:], signed(w_ref[0]), state_ref)

        loop(counts[at] * groups, visit)
        loop(counts[at], keep)

    fine = jnp.max(l_ref[...]) < TOO_LARGE

    @pl.when(jnp.logical_not(fine))
    def _():
        m_ref[...] = mi_ref[...]
        l_ref[...] = li_ref[...]
        acc_ref[...] = ai_ref[...]
        for at in range(parts):
            kv = kv_refs[at]

            def again(index, kv=kv):
                j, t = index // tiles, lax.rem(index, tiles)
                s = dot(qs_ref[t], kv[j, :, :LANES], 1, 1) * unit
                old = m_ref[t]
                new = jnp.maximum(old, jnp.max(s, 1, keepdims=True))
                fade = jnp.exp2(old - new)
                p = jnp.exp2(s - lane_wide(new, keys))
                m_ref[t] = new
                l_ref[t] = l_ref[t] * fade + lane_fold(p)
                acc_ref[t] = acc_ref[t] * fade + dot(p.astype(BF16), kv[j, :, LANES:], 1, 0)

            loop(counts[at] * tiles, again)

    if last:
        lanes = lane_ids((count, LANES))
        for first, out_ref in ((0, mine_ref), (heads, twin_ref)):
            stat = jnp.zeros((count, LANES), F32)
            for h in range(heads):
                t = first + h
                out_ref[h * count:(h + 1) * count, :] = acc_ref[t]
                stat = jnp.where(lanes == h, jnp.sum(l_ref[t], 1, keepdims=True), stat)
                stat = jnp.where(lanes == heads + h, m_ref[t], stat)
            at = heads * count
            out_ref[at:at + count, :] = stat
            out_ref[at + count:at + count + LANES + PAD, :] = state_ref[...]
            out_ref[at + count + LANES + PAD:, :] = near_ref[...]


def folded(grown):
    half = LANES // 2
    turned = grown.T
    return turned[:half] - turned[half:]


def grad_kernel(heads, divisor, qs_ref, kv_ref, w_ref, phik_ref, mine_ref, twin_ref, numer_ref,
                denom_ref, teacher_ref, back_ref, loss_ref, out_ref, gpk_ref, prev_ref):
    count = kv_ref.shape[0]
    at = heads * count
    stat, stat_twin = mine_ref[at:at + count, :], twin_ref[at:at + count, :]
    far, near = at + count, at + count + LANES + PAD
    later_core = jnp.where(lax.axis_index("core") == 1, 1.0, 0.0)
    prev_ref[...] = (
        mine_ref[far:near, :] + twin_ref[far:near, :] + later_core * twin_ref[near:, :]
    )
    back_ref[...] = jnp.zeros_like(back_ref)
    loss_ref[...] = jnp.zeros_like(loss_ref)
    gpk_ref[...] = jnp.zeros_like(gpk_ref)
    first = jnp.where(lane_ids((count, LANES)) == 0, 1.0, 0.0)
    v_more = jnp.concatenate([kv_ref[:, LANES:], first.astype(BF16)], 1)
    allowed = lower_triangle(count)
    turned = lax.broadcasted_iota(jnp.int32, (count, count), 0) <= lane_ids((count, count))
    for h in range(heads):
        m_mine = jnp.broadcast_to(lane_at(stat, heads + h), (count, LANES))
        m_twin = jnp.broadcast_to(lane_at(stat_twin, heads + h), (count, LANES))
        best = jnp.maximum(m_mine, m_twin)
        fade = jnp.exp2(m_mine - best)
        fade_twin = jnp.exp2(m_twin - best)
        total = lane_at(stat, h) * fade + lane_at(stat_twin, h) * fade_twin
        rows = slice(h * count, (h + 1) * count)
        teacher = ((mine_ref[rows, :] * fade + twin_ref[rows, :] * fade_twin) / total).astype(BF16)
        teacher_ref[:, h * LANES:(h + 1) * LANES] = teacher
        q = qs_ref[h]
        phi = feature_map(q, signed(w_ref[h]))
        state = prev_ref[:LANES, :]
        norm = prev_ref[LANES:LANES + 1, :]
        denom = lane_at(denom_ref[...], h) + jnp.sum(phi * norm, 1, keepdims=True)
        rden = 1.0 / denom
        student = (numer_ref[h] + dot_wide(phi, state, 1, 1)) * rden
        err = student - teacher.astype(F32)
        loss_ref[...] += jnp.sum((err * err).reshape(count // EXTRA, EXTRA, LANES), 0)
        g = err * (2.0 / divisor)
        gn = g * rden
        gd = -jnp.sum(g * student, 1, keepdims=True) * rden
        back_ref[:LANES, :] += rows_wide(gn, phi)
        back_ref[LANES:, :] += only_row(jnp.sum(phi * gd, 0, keepdims=True), PAD)
        gn_more = jnp.concatenate([gn, first * gd], 1)
        linked = jnp.where(allowed, dot_exact_right(gn_more, v_more, 1, 1), 0.0)
        linked_t = jnp.where(turned, dot_exact_left(v_more, gn_more, 1, 1), 0.0)
        grad = dot_wide(linked, phik_ref[...], 1, 0) + dot_wide(gn, state, 1, 0) + gd * norm
        gpk_ref[...] += dot_wide(linked_t, phi, 1, 0)
        out_ref[h] = folded(rows_exact(q, feature_pull(phi, grad)))
    loss = jnp.sum(jnp.sum(loss_ref[...], 0, keepdims=True), 1, keepdims=True) * (1.0 / divisor)
    loss_ref[...] = jnp.broadcast_to(loss, (EXTRA, LANES))


def key_kernel(wanted, kv_ref, w_ref, phik_ref, gpk_ref, back_ref, twin_ref, gq_ref, loss_ref,
               *refs):
    parts = len(wanted)
    far_refs, (out_ref, pair_ref, sum_ref) = refs[:parts], refs[parts:]
    pair_ref[...] = back_ref[...] + twin_ref[...]

    def pulled(k, v, phi, of_ref, more, scale):
        grad = dot_exact_left(v, of_ref[:LANES, :], 1, 0) + of_ref[LANES:LANES + 1, :]
        return rows_exact(k, feature_pull(phi, more + scale * grad))

    scale = jnp.where(lax.axis_index("core") == 0, 1.0, 0.0)
    sum_ref[...] = pulled(
        kv_ref[:, :LANES], kv_ref[:, LANES:], phik_ref[...], twin_ref, gpk_ref[...], scale
    )
    for want, far in zip(wanted, far_refs):

        def visit(j, far=far):
            k = far[j, :, :LANES]
            phi = feature_map(k, signed(w_ref[0]))
            sum_ref[...] += pulled(k, far[j, :, LANES:], phi, pair_ref, 0.0, 1.0)

        loop(want(), visit)

    heads, half, _ = gq_ref.shape
    for h in range(heads):
        out_ref[h * half:(h + 1) * half, :] = gq_ref[h]
    at = heads * half
    out_ref[at:at + half, :] = folded(sum_ref[...])
    out_ref[at + half:at + half + EXTRA, :] = loss_ref[...]
    rest = out_ref.shape[0] - at - half - EXTRA
    out_ref[at + half + EXTRA:, :] = jnp.zeros((rest, LANES), F32)


def call(kernel, outs, *args, flops=0, exps=0, limit=16, scratch=(), space=pltpu.VMEM):
    shapes = [jax.ShapeDtypeStruct(shape, kind) for shape, kind in outs]
    moved = sum(math.prod(a.shape) * a.dtype.itemsize for a in list(args) + shapes)
    return pl.pallas_call(
        kernel,
        out_shape=shapes,
        in_specs=[pl.BlockSpec(memory_space=space) for _ in args],
        out_specs=[pl.BlockSpec(memory_space=pltpu.VMEM) for _ in shapes],
        scratch_shapes=list(scratch),
        compiler_params=pltpu.CompilerParams(vmem_limit_bytes=limit << 20),
        cost_estimate=pl.CostEstimate(flops=flops, bytes_accessed=moved, transcendentals=exps),
    )(*args)


def shift(x, axis, by):
    size = lax.axis_size(axis)
    return lax.ppermute(x, axis, [(i, (i + by) % size) for i in range(size)])


def shifts(x, axis):
    return [shift(x, axis, d) for d in range(1, lax.axis_size(axis))]


def swap(x, axis, bit):
    size = lax.axis_size(axis)
    return lax.ppermute(x, axis, [(i, (i ^ bit) % size) for i in range(size)])


def sum_ctx(x, z, y, core):
    steps = (("core", 1, core), ("y", 2, y // 2), ("y", 1, lax.rem(y, 2)))
    part = x
    for axis, bit, mine in steps:
        pieces = part.reshape(2, -1, LANES)
        sent = lax.dynamic_index_in_dim(pieces, 1 - mine, 0, False)
        part = lax.dynamic_index_in_dim(pieces, mine, 0, False) + swap(sent, axis, bit)
    for bit in (1, 2, 4):
        part = part + swap(part, "z", bit)
    for axis, bit, mine in steps[::-1]:
        other = swap(part, axis, bit)
        part = jnp.concatenate(
            [jnp.where(mine == 0, part, other), jnp.where(mine == 0, other, part)]
        )
    return part


def on_device(queries, keys, values, weight_q, weight_k):
    heads, head_dim, half = weight_q.shape
    rows = queries.shape[0]
    unit = math.log2(math.e) / math.sqrt(head_dim)
    z, y, core = (lax.axis_index(name) for name in ("z", "y", "core"))
    wq = jnp.swapaxes(weight_q, 1, 2)
    wk = jnp.swapaxes(weight_k, 1, 2)
    wide = ((heads, rows, head_dim), F32)
    both = ((2 * heads, rows, head_dim), F32)
    slim = ((rows, head_dim), F32)
    state_shape = ((head_dim + PAD, head_dim), F32)
    area = rows * rows * heads

    kv = jnp.concatenate([keys, values], -1)
    qk = jnp.concatenate([queries, keys], -1)
    line = jnp.stack([kv] + shifts(kv, "y"))
    twin = swap(qk, "core", 1)
    line, twin = lax.optimization_barrier((line, twin))

    def paired(bundle):
        return bundle.reshape(NY // 2, 2 * rows, 2 * head_dim)

    qs, *carry, phi_k, state, numer, denom = call(
        functools.partial(near_kernel, heads, unit),
        [((2 * heads, rows, head_dim), BF16)] + [both] * 3 + [slim, state_shape, wide, slim],
        qk, twin, kv, wq, wk, flops=area * head_dim * 18, exps=3 * area,
    )
    carry.append(jnp.zeros_like(state))

    def attend(carry, wanted, parts, last=False):
        keys_each = parts[0].shape[1]
        tokens = sum(part.shape[0] * keys_each for part in parts)
        packed = (((heads + 1) * rows + 2 * state.shape[0], head_dim), F32)
        more = [state] if last else []
        return call(
            functools.partial(far_kernel, heads, unit, wanted, last),
            [packed] * 2 if last else [both] * 3 + [state_shape],
            qs, wk, *carry, *parts, *more,
            flops=2 * rows * heads * tokens * head_dim * 4, exps=2 * rows * heads * tokens,
            scratch=[pltpu.VMEM(*kind) for kind in [both] * 3 + [state_shape]] if last else (),
        )

    per = NY // 2

    def below(step):
        return lambda: jnp.where(lax.axis_index("z") >= step, per, 0)

    held = [line[1:]]
    wanted = [lambda: lax.axis_index("y")]
    carry = attend(carry, wanted, held)
    up, down = shift(line, "z", 1), shift(line, "z", -1)
    for step in range(1, NZ // 2):
        carry, up, down = lax.optimization_barrier((carry, up, down))
        now = [paired(up), paired(down)]
        if step + 1 < NZ // 2:
            up, down = shift(up, "z", 1), shift(down, "z", -1)
        else:
            across = [shift(up[:per], "z", 1), shift(down[per:], "z", -1)]
        held += now
        wanted += [below(step), below(NZ - step)]
        carry = attend(carry, wanted[-2:], now)
    held.append(paired(jnp.concatenate(across)))
    wanted.append(below(NZ // 2))
    mine, pack = attend(carry, wanted[-1:], held[-1:], last=True)
    pack = swap(pack, "core", 1)

    places = NY * NCORE
    divisor = float(rows * NZ * places * heads * lax.axis_size("head"))
    teacher, back, loss, grown_q, gpk = call(
        functools.partial(grad_kernel, heads, divisor),
        [
            ((rows, heads * head_dim), BF16), state_shape, ((EXTRA, head_dim), F32),
            ((heads, half, head_dim), F32), slim,
        ],
        qs, kv, wq, phi_k, mine, pack, numer, denom,
        flops=area * head_dim * 30, scratch=[pltpu.VMEM(*state_shape)],
    )
    twin_back = swap(back, "core", 1)
    for bit in (1, 2):
        loss = loss + swap(loss, "head", bit)
    q_rows = heads * half
    depth = -(-(q_rows + half + EXTRA) // (places * EXTRA)) * EXTRA
    (grown,) = call(
        functools.partial(key_kernel, wanted), [((places * depth, head_dim), F32)],
        kv, wk, phi_k, gpk, back, twin_back, grown_q, loss, *held,
        flops=rows * head_dim * head_dim * 10 * NZ * NY, limit=24,
        scratch=[pltpu.VMEM(*state_shape), pltpu.VMEM((head_dim, head_dim), F32)],
    )
    summed = sum_ctx(grown, z, y, core)
    grad_q = summed[:q_rows].reshape(heads, half, head_dim)
    grad_k = summed[q_rows:q_rows + half].reshape(1, half, head_dim)
    loss = summed[q_rows + half, 0]
    return (teacher, loss, jnp.swapaxes(grad_q, 1, 2), jnp.swapaxes(grad_k, 1, 2))


def solution(mesh):
    grid = Mesh(
        mesh.devices.reshape(NZ, NY, NCORE, mesh.devices.shape[1]), ("z", "y", "core", "head")
    )
    ctx = ("z", "y", "core")
    placed = (
        P(ctx, "head"),
        P(ctx, "head"),
        P(ctx, "head"),
        P("head", None, None),
        P("head", None, None),
    )
    return jax.shard_map(
        on_device,
        mesh=grid,
        in_specs=placed,
        out_specs=(P(ctx, "head"), P(), P("head", None, None), P("head", None, None)),
        check_vma=False,
    )
```

```python
import functools
import math

import jax
import jax.numpy as jnp
from jax import lax
from jax.experimental import pallas as pl
from jax.experimental.pallas import tpu as pltpu
from jax.sharding import Mesh, PartitionSpec as P

F32 = jnp.float32
BF16 = jnp.bfloat16
NEGATIVE = -1e30
TOO_LARGE = 2.0 ** 100
FINITE = 3.3e38
LANES = 128
EXTRA = 8
PAD = 16
NZ, NY, NCORE = 8, 4, 2


def dot(a, b, ca, cb):
    return lax.dot_general(a, b, (((ca,), (cb,)), ((), ())), preferred_element_type=F32)


def split(x):
    high = x.astype(BF16)
    return high, (x - high.astype(F32)).astype(BF16)


def dot_exact_right(x, e, cx, ce):
    high, low = split(x)
    return dot(high, e, cx, ce) + dot(low, e, cx, ce)


def dot_exact_left(e, x, ce, cx):
    high, low = split(x)
    return dot(e, high, ce, cx) + dot(e, low, ce, cx)


def dot_wide(x, y, cx, cy):
    xh, xl = split(x)
    yh, yl = split(y)
    return dot(xh, yh, cx, cy) + (dot(xh, yl, cx, cy) + dot(xl, yh, cx, cy))


def side_by_side(x):
    return jnp.concatenate(split(x), 1)


def halves_added(x):
    half = x.shape[1] // 2
    return x[:, :half] + x[:, half:]


def rows_exact(e, x):
    return halves_added(dot(e, side_by_side(x), 0, 0))


def rows_wide(x, y):
    both = halves_added(dot(side_by_side(x), side_by_side(y), 0, 0))
    half = both.shape[0] // 2
    return both[:half] + both[half:]


def lane_ids(shape):
    return lax.broadcasted_iota(jnp.int32, shape, 1)


def half_ones(depth):
    rows = lax.broadcasted_iota(jnp.int32, (depth, LANES), 0) & (LANES // 2)
    cols = lane_ids((depth, LANES)) & (LANES // 2)
    return jnp.where(rows == cols, 1.0, 0.0).astype(BF16)


def half_sums(high, low):
    return dot(jnp.concatenate([high, low], 1), half_ones(2 * LANES), 1, 0)


def feature_map(x, w2):
    e = jnp.exp(dot(x, w2, 1, 1))
    high = jnp.minimum(e, FINITE).astype(BF16)
    return e / half_sums(high, (e - high.astype(F32)).astype(BF16))


def signed(w):
    return jnp.concatenate([w, -w], 0)


def feature_pull(phi, grad):
    return phi * (grad - half_sums(*split(phi * grad)))


def row_total(x):
    return jnp.broadcast_to(jnp.sum(x, 1, keepdims=True), (x.shape[0], LANES))


def lane_wide(x, width):
    return jnp.concatenate([x] * (width // LANES), 1)


def lane_at(x, lane):
    return jnp.sum(jnp.where(lane_ids(x.shape) == lane, x, 0.0), 1, keepdims=True)


def lower_triangle(count):
    rows = lax.broadcasted_iota(jnp.int32, (count, count), 0)
    return lane_ids((count, count)) <= rows


def only_row(row, count):
    at = lax.broadcasted_iota(jnp.int32, (count, LANES), 0)
    return jnp.where(at == 0, row, 0.0)


def loop(count, body):
    def visit(index, unused):
        body(index)
        return unused

    lax.fori_loop(0, count, visit, 0)


def add_state(k, v, phi, state_ref):
    state_ref[:LANES, :] += rows_exact(v, phi)
    state_ref[LANES:, :] += only_row(jnp.sum(phi, 0, keepdims=True), PAD)


def near_kernel(heads, unit, q_ref, twin_ref, twin_k_ref, kv_ref, wq_ref, wk_ref, qs_ref,
                m_ref, l_ref, acc_ref, phik_ref, state_ref, numer_ref, denom_ref):
    count = kv_ref.shape[0]
    v = kv_ref[:, LANES:]
    state_ref[...] = jnp.zeros_like(state_ref)
    denom_ref[...] = jnp.zeros_like(denom_ref)
    k = kv_ref[:, :LANES]
    phi_k = feature_map(k, signed(wk_ref[0]))
    phik_ref[...] = phi_k
    add_state(k, v, phi_k, state_ref)
    for h in range(heads):
        qs_ref[h] = q_ref[:, h * LANES:(h + 1) * LANES]
        qs_ref[heads + h] = twin_ref[:, h * LANES:(h + 1) * LANES]

    def head(h):
        allowed = lower_triangle(count)
        q = qs_ref[h]
        s = jnp.where(allowed, dot(q, kv_ref[:, :LANES], 1, 1) * unit, NEGATIVE)
        best = jnp.max(s, 1, keepdims=True)
        p = jnp.exp2(s - best)
        m_ref[h] = jnp.broadcast_to(best, (count, LANES))
        l_ref[h] = row_total(p)
        acc_ref[h] = dot(p.astype(BF16), v, 1, 0)
        s = jnp.where(allowed, dot(qs_ref[heads + h], twin_k_ref[...], 1, 1) * unit, NEGATIVE)
        m_ref[heads + h] = jnp.broadcast_to(jnp.max(s, 1, keepdims=True), (count, LANES))
        l_ref[heads + h] = jnp.zeros((count, LANES), F32)
        acc_ref[heads + h] = jnp.zeros((count, LANES), F32)
        phi = feature_map(q, signed(wq_ref[h]))
        scores = jnp.where(allowed, dot_wide(phi, phik_ref[...], 1, 1), 0.0)
        numer_ref[h] = dot_exact_right(scores, v, 1, 0)
        denom_ref[...] = jnp.where(
            lane_ids((count, LANES)) == h, jnp.sum(scores, 1, keepdims=True), denom_ref[...]
        )

    loop(heads, head)

    def twin_head(h):
        at = heads + h
        s = dot(qs_ref[at], kv_ref[:, :LANES], 1, 1) * unit
        new = jnp.maximum(m_ref[at], jnp.max(s, 1, keepdims=True))
        p = jnp.exp2(s - lane_wide(new, count))
        m_ref[at] = new
        l_ref[at] = row_total(p)
        acc_ref[at] = dot(p.astype(BF16), v, 1, 0)

    loop(jnp.where(lax.axis_index("core") == 0, heads, 0), twin_head)


def far_kernel(heads, unit, wanted, last, qs_ref, w_ref, mi_ref, li_ref, ai_ref, si_ref, *refs):
    parts = len(wanted)
    kv_refs, refs, chunk_ref = refs[:parts], refs[parts:-1], refs[-1]
    if last:
        near_ref, mine_ref, twin_ref, m_ref, l_ref, acc_ref, state_ref = refs
    else:
        m_ref, l_ref, acc_ref, state_ref = refs
    counts = [want() for want in wanted]
    tiles, count, _ = qs_ref.shape
    keys = kv_refs[0].shape[1]
    m_ref[...] = mi_ref[...]
    l_ref[...] = li_ref[...]
    acc_ref[...] = ai_ref[...]
    state_ref[...] = si_ref[...]

    def visit(index):
        ahead = 0
        for number, kv in zip(counts, kv_refs):

            @pl.when((index >= ahead) & (index < ahead + number))
            def _(kv=kv, ahead=ahead):
                chunk_ref[...] = kv[index - ahead]

            ahead = ahead + number
        k = chunk_ref[:, :LANES]
        v = jnp.concatenate([chunk_ref[:, LANES:], jnp.ones((keys, LANES), BF16)], 1)
        following = dot(qs_ref[0], k, 1, 1)
        for t in range(tiles):
            s = following
            if t + 1 < tiles:
                following = dot(qs_ref[t + 1], k, 1, 1)
            p = jnp.exp2(s * unit - lane_wide(m_ref[t], keys))
            grown = dot(p.astype(BF16), v, 1, 0)
            acc_ref[t] += grown[:, :LANES]
            l_ref[t] += grown[:, LANES:]
        add_state(k, chunk_ref[:, LANES:], feature_map(k, signed(w_ref[0])), state_ref)

    loop(sum(counts), visit)

    fine = jnp.max(l_ref[...]) < TOO_LARGE

    @pl.when(jnp.logical_not(fine))
    def _():
        m_ref[...] = mi_ref[...]
        l_ref[...] = li_ref[...]
        acc_ref[...] = ai_ref[...]
        for at in range(parts):
            kv = kv_refs[at]

            def again(index, kv=kv):
                j, t = index // tiles, lax.rem(index, tiles)
                s = dot(qs_ref[t], kv[j, :, :LANES], 1, 1) * unit
                old = m_ref[t]
                new = jnp.maximum(old, jnp.max(s, 1, keepdims=True))
                fade = jnp.exp2(old - new)
                p = jnp.exp2(s - lane_wide(new, keys))
                m_ref[t] = new
                l_ref[t] = l_ref[t] * fade + row_total(p)
                acc_ref[t] = acc_ref[t] * fade + dot(p.astype(BF16), kv[j, :, LANES:], 1, 0)

            loop(counts[at] * tiles, again)

    if last:
        lanes = lane_ids((count, LANES))
        for first, out_ref in ((0, mine_ref), (heads, twin_ref)):
            stat = jnp.zeros((count, LANES), F32)
            for h in range(heads):
                t = first + h
                out_ref[h * count:(h + 1) * count, :] = acc_ref[t]
                stat = jnp.where(lanes == h, l_ref[t], stat)
                stat = jnp.where(lanes == heads + h, m_ref[t], stat)
            at = heads * count
            out_ref[at:at + count, :] = stat
            out_ref[at + count:at + count + LANES + PAD, :] = state_ref[...]
            out_ref[at + count + LANES + PAD:, :] = near_ref[...]


def folded(grown):
    half = LANES // 2
    turned = grown.T
    return turned[:half] - turned[half:]


def grad_kernel(heads, divisor, qs_ref, kv_ref, w_ref, phik_ref, mine_ref, twin_ref, numer_ref,
                denom_ref, teacher_ref, back_ref, loss_ref, out_ref, gpk_ref, prev_ref):
    count = kv_ref.shape[0]
    at = heads * count
    stat, stat_twin = mine_ref[at:at + count, :], twin_ref[at:at + count, :]
    far, near = at + count, at + count + LANES + PAD
    later_core = jnp.where(lax.axis_index("core") == 1, 1.0, 0.0)
    prev_ref[...] = (
        mine_ref[far:near, :] + twin_ref[far:near, :] + later_core * twin_ref[near:, :]
    )
    back_ref[...] = jnp.zeros_like(back_ref)
    loss_ref[...] = jnp.zeros_like(loss_ref)
    gpk_ref[...] = jnp.zeros_like(gpk_ref)
    first = jnp.where(lane_ids((count, LANES)) == 0, 1.0, 0.0)
    phi_k = phik_ref[...].astype(BF16)
    v_more = jnp.concatenate([kv_ref[:, LANES:], first.astype(BF16)], 1)
    allowed = lower_triangle(count)
    turned = lax.broadcasted_iota(jnp.int32, (count, count), 0) <= lane_ids((count, count))
    for h in range(heads):
        m_mine = jnp.broadcast_to(lane_at(stat, heads + h), (count, LANES))
        m_twin = jnp.broadcast_to(lane_at(stat_twin, heads + h), (count, LANES))
        best = jnp.maximum(m_mine, m_twin)
        fade = jnp.exp2(m_mine - best)
        fade_twin = jnp.exp2(m_twin - best)
        total = lane_at(stat, h) * fade + lane_at(stat_twin, h) * fade_twin
        rows = slice(h * count, (h + 1) * count)
        teacher = ((mine_ref[rows, :] * fade + twin_ref[rows, :] * fade_twin) / total).astype(BF16)
        teacher_ref[:, h * LANES:(h + 1) * LANES] = teacher
        q = qs_ref[h]
        phi = feature_map(q, signed(w_ref[h]))
        state = prev_ref[:LANES, :]
        norm = prev_ref[LANES:LANES + 1, :]
        denom = lane_at(denom_ref[...], h) + jnp.sum(phi * norm, 1, keepdims=True)
        rden = 1.0 / denom
        student = (numer_ref[h] + dot_wide(phi, state, 1, 1)) * rden
        err = student - teacher.astype(F32)
        loss_ref[...] += jnp.sum((err * err).reshape(count // EXTRA, EXTRA, LANES), 0)
        g = err * (2.0 / divisor)
        gn = g * rden
        gd = -jnp.sum(g * student, 1, keepdims=True) * rden
        back_ref[:LANES, :] += rows_wide(gn, phi)
        back_ref[LANES:, :] += only_row(jnp.sum(phi * gd, 0, keepdims=True), PAD)
        gn_more = jnp.concatenate([gn, first * gd], 1)
        linked = jnp.where(allowed, dot_exact_right(gn_more, v_more, 1, 1), 0.0)
        linked_t = jnp.where(turned, dot_exact_left(v_more, gn_more, 1, 1), 0.0)
        grad = dot(linked.astype(BF16), phi_k, 1, 0) + dot_wide(gn, state, 1, 0) + gd * norm
        gpk_ref[...] += dot(linked_t.astype(BF16), phi.astype(BF16), 1, 0)
        out_ref[h] = folded(rows_exact(q, feature_pull(phi, grad)))
    loss = jnp.sum(jnp.sum(loss_ref[...], 0, keepdims=True), 1, keepdims=True) * (1.0 / divisor)
    loss_ref[...] = jnp.broadcast_to(loss, (EXTRA, LANES))


def key_kernel(wanted, kv_ref, w_ref, phik_ref, gpk_ref, back_ref, twin_ref, gq_ref, *refs):
    parts = len(wanted)
    held, refs = refs[-parts:], refs[:-parts]
    out_ref, pair_ref, sum_ref, flat_ref, sems = refs[-5:]
    far_refs, losses = refs[-parts - 5:-5], refs[:-parts - 5]
    loss = sum(ref[...] for ref in losses[0::2]) + sum(ref[...] for ref in losses[1::2])
    counts = [want() for want in wanted]
    copies = [
        pltpu.make_async_copy(far, here, sems.at[at])
        for at, (far, here) in enumerate(zip(far_refs, held))
    ]
    for number, copy in zip(counts, copies):
        pl.when(number > 0)(copy.start)
    pair_ref[...] = back_ref[...] + twin_ref[...]

    def pulled(k, v, phi, of_ref, more, scale):
        grad = halves_added(dot(v, side_by_side(of_ref[:LANES, :]), 1, 0))
        grad = grad + of_ref[LANES:LANES + 1, :]
        return rows_exact(k, feature_pull(phi, more + scale * grad))

    scale = jnp.where(lax.axis_index("core") == 0, 1.0, 0.0)
    sum_ref[...] = pulled(
        kv_ref[:, :LANES], kv_ref[:, LANES:], phik_ref[...], twin_ref, gpk_ref[...], scale
    )
    for number, copy, here in zip(counts, copies, held):

        def visit(j, here=here):
            k = here[j, :, :LANES]
            phi = feature_map(k, signed(w_ref[0]))
            sum_ref[...] += pulled(k, here[j, :, LANES:], phi, pair_ref, 0.0, 1.0)

        pl.when(number > 0)(copy.wait)
        loop(number, visit)

    heads, half, _ = gq_ref.shape
    for h in range(heads):
        flat_ref[h * half:(h + 1) * half, :] = gq_ref[h]
    flat_ref[heads * half:, :] = folded(sum_ref[...])
    slices, depth, _ = out_ref.shape
    depth -= EXTRA
    for at in range(slices):
        out_ref[at, :depth, :] = flat_ref[at * depth:(at + 1) * depth, :]
        out_ref[at, depth:, :] = loss


def call(kernel, outs, *args, flops=0, exps=0, limit=16, scratch=(), away=0):
    shapes = [jax.ShapeDtypeStruct(shape, kind) for shape, kind in outs]
    moved = sum(math.prod(a.shape) * a.dtype.itemsize for a in list(args) + shapes)
    spaces = [pltpu.VMEM] * (len(args) - away) + [pl.ANY] * away
    return pl.pallas_call(
        kernel,
        out_shape=shapes,
        in_specs=[pl.BlockSpec(memory_space=space) for space in spaces],
        out_specs=[pl.BlockSpec(memory_space=pltpu.VMEM) for _ in shapes],
        scratch_shapes=list(scratch),
        compiler_params=pltpu.CompilerParams(vmem_limit_bytes=limit << 20),
        cost_estimate=pl.CostEstimate(flops=flops, bytes_accessed=moved, transcendentals=exps),
    )(*args)


def shift(x, axis, by):
    size = lax.axis_size(axis)
    return lax.ppermute(x, axis, [(i, (i + by) % size) for i in range(size)])


def shifts(x, axis):
    return [shift(x, axis, d) for d in range(1, lax.axis_size(axis))]


def swap(x, axis, bit):
    size = lax.axis_size(axis)
    return lax.ppermute(x, axis, [(i, (i ^ bit) % size) for i in range(size)])


def in_order(pieces, mine):
    count = len(pieces)
    return jnp.stack(
        [lax.select_n(lax.rem(mine - at + count, count), *pieces) for at in range(count)]
    )


def sum_ctx(x, y, core):
    pieces = x.reshape((NCORE, NY) + x.shape[1:])
    sent = lax.dynamic_index_in_dim(pieces, 1 - core, 0, False)
    part = lax.dynamic_index_in_dim(pieces, core, 0, False) + swap(sent, "core", 1)
    held = lax.dynamic_index_in_dim(part, y, 0, False)
    for d in range(1, NY):
        sent = lax.dynamic_index_in_dim(part, lax.rem(y + d, NY), 0, False)
        held = held + shift(sent, "y", d)
    held = held + swap(held, "z", 1)
    ahead, opposite, behind = (shift(held, "z", d) for d in (2, 4, 6))
    held = (held + opposite) + (ahead + behind)
    loss = held[-EXTRA, 0]
    held = held[:-EXTRA]
    mine = in_order([held] + shifts(held, "y"), y)
    other = swap(mine, "core", 1)
    both = [jnp.where(core == 0, mine, other), jnp.where(core == 0, other, mine)]
    return jnp.concatenate(both).reshape(-1, LANES), loss


def on_device(queries, keys, values, weight_q, weight_k):
    heads, head_dim, half = weight_q.shape
    rows = queries.shape[0]
    unit = math.log2(math.e) / math.sqrt(head_dim)
    z, y, core = (lax.axis_index(name) for name in ("z", "y", "core"))
    wq = jnp.swapaxes(weight_q, 1, 2)
    wk = jnp.swapaxes(weight_k, 1, 2)
    wide = ((heads, rows, head_dim), F32)
    both = ((2 * heads, rows, head_dim), F32)
    slim = ((rows, head_dim), F32)
    state_shape = ((head_dim + PAD, head_dim), F32)
    area = rows * rows * heads

    kv = jnp.concatenate([keys, values], -1)
    line = jnp.stack([kv] + shifts(kv, "y"))
    twin = swap(queries, "core", 1)
    twin_k = swap(keys, "core", 1)
    line, twin, twin_k = lax.optimization_barrier((line, twin, twin_k))

    def paired(bundle):
        return bundle.reshape(NY // 2, 2 * rows, 2 * head_dim)

    qs, *carry, phi_k, state, numer, denom = call(
        functools.partial(near_kernel, heads, unit),
        [((2 * heads, rows, head_dim), BF16)] + [both] * 3 + [slim, state_shape, wide, slim],
        queries, twin, twin_k, kv, wq, wk, flops=area * head_dim * 18, exps=3 * area,
    )
    carry.append(jnp.zeros_like(state))

    def attend(carry, wanted, parts, last=False):
        keys_each = parts[0].shape[1]
        tokens = sum(part.shape[0] * keys_each for part in parts)
        packed = (((heads + 1) * rows + 2 * state.shape[0], head_dim), F32)
        more = [state] if last else []
        return call(
            functools.partial(far_kernel, heads, unit, wanted, last),
            [packed] * 2 if last else [both] * 3 + [state_shape],
            qs, wk, *carry, *parts, *more,
            flops=2 * rows * heads * tokens * head_dim * 4, exps=2 * rows * heads * tokens,
            scratch=[pltpu.VMEM(*kind) for kind in ([both] * 3 + [state_shape] if last else [])]
            + [pltpu.VMEM(parts[0].shape[1:], BF16)],
        )

    per = NY // 2

    def below(step):
        return lambda: jnp.where(lax.axis_index("z") >= step, per, 0)

    held = [line[1:]]
    wanted = [lambda: lax.axis_index("y")]
    carry = attend(carry, wanted, held)
    up, down = shift(line, "z", 1), shift(line, "z", -1)
    for step in range(1, NZ // 2):
        carry, up, down = lax.optimization_barrier((carry, up, down))
        now = [paired(up), paired(down)]
        if step + 1 < NZ // 2:
            up, down = shift(up, "z", 1), shift(down, "z", -1)
        else:
            across = [shift(up[:per], "z", 1), shift(down[per:], "z", -1)]
        held += now
        wanted += [below(step), below(NZ - step)]
        carry = attend(carry, wanted[-2:], now)
    held.append(paired(jnp.concatenate(across)))
    wanted.append(below(NZ // 2))
    mine, pack = attend(carry, wanted[-1:], held[-1:], last=True)
    pack = swap(pack, "core", 1)

    places = NY * NCORE
    divisor = float(rows * NZ * places * heads * lax.axis_size("head"))
    teacher, back, loss, grown_q, gpk = call(
        functools.partial(grad_kernel, heads, divisor),
        [
            ((rows, heads * head_dim), BF16), state_shape, ((EXTRA, head_dim), F32),
            ((heads, half, head_dim), F32), slim,
        ],
        qs, kv, wq, phi_k, mine, pack, numer, denom,
        flops=area * head_dim * 30, scratch=[pltpu.VMEM(*state_shape)],
    )
    twin_back = swap(back, "core", 1)
    by_head = [loss] + shifts(loss, "head")
    q_rows = heads * half
    flat = (q_rows + half, head_dim)
    (grown,) = call(
        functools.partial(key_kernel, wanted),
        [((places, flat[0] // places + EXTRA, head_dim), F32)],
        kv, wk, phi_k, gpk, back, twin_back, grown_q, *by_head, *held,
        flops=rows * head_dim * head_dim * 10 * NZ * NY, limit=48, away=len(held),
        scratch=[
            pltpu.VMEM(*state_shape), pltpu.VMEM((head_dim, head_dim), F32),
            pltpu.VMEM(flat, F32), pltpu.SemaphoreType.DMA((len(held),)),
        ] + [pltpu.VMEM(part.shape, BF16) for part in held],
    )
    summed, loss = sum_ctx(grown, y, core)
    grad_q = summed[:q_rows].reshape(heads, half, head_dim)
    grad_k = summed[q_rows:].reshape(1, half, head_dim)
    return (teacher, loss, jnp.swapaxes(grad_q, 1, 2), jnp.swapaxes(grad_k, 1, 2))


def solution(mesh):
    grid = Mesh(
        mesh.devices.reshape(NZ, NY, NCORE, mesh.devices.shape[1]), ("z", "y", "core", "head")
    )
    ctx = ("z", "y", "core")
    placed = (
        P(ctx, "head"),
        P(ctx, "head"),
        P(ctx, "head"),
        P("head", None, None),
        P("head", None, None),
    )
    return jax.shard_map(
        on_device,
        mesh=grid,
        in_specs=placed,
        out_specs=(P(ctx, "head"), P(), P("head", None, None), P("head", None, None)),
        check_vma=False,
    )
```

```python
import functools
import math

import jax
import jax.numpy as jnp
from jax import lax
from jax.experimental import pallas as pl
from jax.experimental.pallas import tpu as pltpu
from jax.sharding import Mesh, PartitionSpec as P

F32 = jnp.float32
BF16 = jnp.bfloat16
NEGATIVE = -1e30
TOO_LARGE = 2.0 ** 100
FINITE = 3.3e38
LANES = 128
EXTRA = 8
PAD = 16
NZ, NY, NCORE = 8, 4, 2


def dot(a, b, ca, cb):
    return lax.dot_general(a, b, (((ca,), (cb,)), ((), ())), preferred_element_type=F32)


def split(x):
    high = x.astype(BF16)
    return high, (x - high.astype(F32)).astype(BF16)


def dot_exact_right(x, e, cx, ce):
    high, low = split(x)
    return dot(high, e, cx, ce) + dot(low, e, cx, ce)


def dot_exact_left(e, x, ce, cx):
    high, low = split(x)
    return dot(e, high, ce, cx) + dot(e, low, ce, cx)


def dot_wide(x, y, cx, cy):
    xh, xl = split(x)
    yh, yl = split(y)
    return dot(xh, yh, cx, cy) + (dot(xh, yl, cx, cy) + dot(xl, yh, cx, cy))


def side_by_side(x):
    return jnp.concatenate(split(x), 1)


def halves_added(x):
    half = x.shape[1] // 2
    return x[:, :half] + x[:, half:]


def rows_exact(e, x):
    return halves_added(dot(e, side_by_side(x), 0, 0))


def rows_wide(x, y):
    both = halves_added(dot(side_by_side(x), side_by_side(y), 0, 0))
    half = both.shape[0] // 2
    return both[:half] + both[half:]


def lane_ids(shape):
    return lax.broadcasted_iota(jnp.int32, shape, 1)


def half_ones(depth):
    rows = lax.broadcasted_iota(jnp.int32, (depth, LANES), 0) & (LANES // 2)
    cols = lane_ids((depth, LANES)) & (LANES // 2)
    return jnp.where(rows == cols, 1.0, 0.0).astype(BF16)


def half_sums(high, low):
    return dot(jnp.concatenate([high, low], 1), half_ones(2 * LANES), 1, 0)


def feature_map(x, w2):
    e = jnp.exp(dot(x, w2, 1, 1))
    high = jnp.minimum(e, FINITE).astype(BF16)
    return e / half_sums(high, (e - high.astype(F32)).astype(BF16))


def signed(w):
    return jnp.concatenate([w, -w], 0)


def feature_pull(phi, grad):
    return phi * (grad - half_sums(*split(phi * grad)))


def row_total(x):
    return jnp.broadcast_to(jnp.sum(x, 1, keepdims=True), (x.shape[0], LANES))


def lane_wide(x, width):
    return jnp.concatenate([x] * (width // LANES), 1)


def lane_at(x, lane):
    return jnp.sum(jnp.where(lane_ids(x.shape) == lane, x, 0.0), 1, keepdims=True)


def lower_triangle(count):
    rows = lax.broadcasted_iota(jnp.int32, (count, count), 0)
    return lane_ids((count, count)) <= rows


def only_row(row, count):
    at = lax.broadcasted_iota(jnp.int32, (count, LANES), 0)
    return jnp.where(at == 0, row, 0.0)


def loop(count, body):
    def visit(index, unused):
        body(index)
        return unused

    lax.fori_loop(0, count, visit, 0)


def add_state(k, v, phi, state_ref):
    state_ref[:LANES, :] += rows_exact(v, phi)
    state_ref[LANES:, :] += only_row(jnp.sum(phi, 0, keepdims=True), PAD)


def near_kernel(heads, unit, q_ref, twin_ref, twin_k_ref, kv_ref, wq_ref, wk_ref, qs_ref,
                m_ref, l_ref, acc_ref, phik_ref, state_ref, numer_ref, denom_ref):
    count = kv_ref.shape[0]
    v = kv_ref[:, LANES:]
    state_ref[...] = jnp.zeros_like(state_ref)
    denom_ref[...] = jnp.zeros_like(denom_ref)
    k = kv_ref[:, :LANES]
    phi_k = feature_map(k, signed(wk_ref[0]))
    phik_ref[...] = phi_k
    add_state(k, v, phi_k, state_ref)
    for h in range(heads):
        qs_ref[h] = q_ref[:, h * LANES:(h + 1) * LANES]
        qs_ref[heads + h] = twin_ref[:, h * LANES:(h + 1) * LANES]

    def head(h):
        allowed = lower_triangle(count)
        q = qs_ref[h]
        s = jnp.where(allowed, dot(q, kv_ref[:, :LANES], 1, 1) * unit, NEGATIVE)
        best = jnp.max(s, 1, keepdims=True)
        p = jnp.exp2(s - best)
        m_ref[h] = jnp.broadcast_to(best, (count, LANES))
        l_ref[h] = row_total(p)
        acc_ref[h] = dot(p.astype(BF16), v, 1, 0)
        s = jnp.where(allowed, dot(qs_ref[heads + h], twin_k_ref[...], 1, 1) * unit, NEGATIVE)
        m_ref[heads + h] = jnp.broadcast_to(jnp.max(s, 1, keepdims=True), (count, LANES))
        l_ref[heads + h] = jnp.zeros((count, LANES), F32)
        acc_ref[heads + h] = jnp.zeros((count, LANES), F32)
        phi = feature_map(q, signed(wq_ref[h]))
        scores = jnp.where(allowed, dot_wide(phi, phik_ref[...], 1, 1), 0.0)
        numer_ref[h] = dot_exact_right(scores, v, 1, 0)
        denom_ref[...] = jnp.where(
            lane_ids((count, LANES)) == h, jnp.sum(scores, 1, keepdims=True), denom_ref[...]
        )

    loop(heads, head)

    def twin_head(h):
        at = heads + h
        s = dot(qs_ref[at], kv_ref[:, :LANES], 1, 1) * unit
        new = jnp.maximum(m_ref[at], jnp.max(s, 1, keepdims=True))
        p = jnp.exp2(s - lane_wide(new, count))
        m_ref[at] = new
        l_ref[at] = row_total(p)
        acc_ref[at] = dot(p.astype(BF16), v, 1, 0)

    loop(jnp.where(lax.axis_index("core") == 0, heads, 0), twin_head)


def far_kernel(heads, unit, wanted, last, qs_ref, w_ref, mi_ref, li_ref, ai_ref, si_ref, *refs):
    parts = len(wanted)
    kv_refs, refs, chunk_ref = refs[:parts], refs[parts:-1], refs[-1]
    if last:
        near_ref, mine_ref, twin_ref, m_ref, l_ref, acc_ref, state_ref = refs
    else:
        m_ref, l_ref, acc_ref, state_ref = refs
    counts = [want() for want in wanted]
    tiles, count, _ = qs_ref.shape
    keys = kv_refs[0].shape[1]
    m_ref[...] = mi_ref[...]
    l_ref[...] = li_ref[...]
    acc_ref[...] = ai_ref[...]
    state_ref[...] = si_ref[...]

    def visit(index):
        ahead = 0
        for number, kv in zip(counts, kv_refs):

            @pl.when((index >= ahead) & (index < ahead + number))
            def _(kv=kv, ahead=ahead):
                chunk_ref[...] = kv[index - ahead]

            ahead = ahead + number
        k = chunk_ref[:, :LANES]
        v = jnp.concatenate([chunk_ref[:, LANES:], jnp.ones((keys, LANES), BF16)], 1)
        following = dot(qs_ref[0], k, 1, 1)
        for t in range(tiles):
            s = following
            if t + 1 < tiles:
                following = dot(qs_ref[t + 1], k, 1, 1)
            p = jnp.exp2(s * unit - lane_wide(m_ref[t], keys))
            grown = dot(p.astype(BF16), v, 1, 0)
            acc_ref[t] += grown[:, :LANES]
            l_ref[t] += grown[:, LANES:]
        add_state(k, chunk_ref[:, LANES:], feature_map(k, signed(w_ref[0])), state_ref)

    loop(sum(counts), visit)

    fine = jnp.max(l_ref[...]) < TOO_LARGE

    @pl.when(jnp.logical_not(fine))
    def _():
        m_ref[...] = mi_ref[...]
        l_ref[...] = li_ref[...]
        acc_ref[...] = ai_ref[...]
        for at in range(parts):
            kv = kv_refs[at]

            def again(index, kv=kv):
                j, t = index // tiles, lax.rem(index, tiles)
                s = dot(qs_ref[t], kv[j, :, :LANES], 1, 1) * unit
                old = m_ref[t]
                new = jnp.maximum(old, jnp.max(s, 1, keepdims=True))
                fade = jnp.exp2(old - new)
                p = jnp.exp2(s - lane_wide(new, keys))
                m_ref[t] = new
                l_ref[t] = l_ref[t] * fade + row_total(p)
                acc_ref[t] = acc_ref[t] * fade + dot(p.astype(BF16), kv[j, :, LANES:], 1, 0)

            loop(counts[at] * tiles, again)

    if last:
        lanes = lane_ids((count, LANES))
        for first, out_ref in ((0, mine_ref), (heads, twin_ref)):
            stat = jnp.zeros((count, LANES), F32)
            for h in range(heads):
                t = first + h
                out_ref[h * count:(h + 1) * count, :] = acc_ref[t]
                stat = jnp.where(lanes == h, l_ref[t], stat)
                stat = jnp.where(lanes == heads + h, m_ref[t], stat)
            at = heads * count
            out_ref[at:at + count, :] = stat
            out_ref[at + count:at + count + LANES + PAD, :] = state_ref[...]
            out_ref[at + count + LANES + PAD:, :] = near_ref[...]


def folded(grown):
    half = LANES // 2
    turned = grown.T
    return turned[:half] - turned[half:]


def grad_kernel(heads, divisor, qs_ref, kv_ref, w_ref, phik_ref, mine_ref, twin_ref, numer_ref,
                denom_ref, teacher_ref, back_ref, loss_ref, out_ref, gpk_ref, prev_ref):
    count = kv_ref.shape[0]
    at = heads * count
    stat, stat_twin = mine_ref[at:at + count, :], twin_ref[at:at + count, :]
    far, near = at + count, at + count + LANES + PAD
    later_core = jnp.where(lax.axis_index("core") == 1, 1.0, 0.0)
    prev_ref[...] = (
        mine_ref[far:near, :] + twin_ref[far:near, :] + later_core * twin_ref[near:, :]
    )
    back_ref[...] = jnp.zeros_like(back_ref)
    loss_ref[...] = jnp.zeros_like(loss_ref)
    gpk_ref[...] = jnp.zeros_like(gpk_ref)
    first = jnp.where(lane_ids((count, LANES)) == 0, 1.0, 0.0)
    v_more = jnp.concatenate([kv_ref[:, LANES:], first.astype(BF16)], 1)
    allowed = lower_triangle(count)
    turned = lax.broadcasted_iota(jnp.int32, (count, count), 0) <= lane_ids((count, count))
    for h in range(heads):
        m_mine = jnp.broadcast_to(lane_at(stat, heads + h), (count, LANES))
        m_twin = jnp.broadcast_to(lane_at(stat_twin, heads + h), (count, LANES))
        best = jnp.maximum(m_mine, m_twin)
        fade = jnp.exp2(m_mine - best)
        fade_twin = jnp.exp2(m_twin - best)
        total = lane_at(stat, h) * fade + lane_at(stat_twin, h) * fade_twin
        rows = slice(h * count, (h + 1) * count)
        teacher = ((mine_ref[rows, :] * fade + twin_ref[rows, :] * fade_twin) / total).astype(BF16)
        teacher_ref[:, h * LANES:(h + 1) * LANES] = teacher
        q = qs_ref[h]
        phi = feature_map(q, signed(w_ref[h]))
        state = prev_ref[:LANES, :]
        norm = prev_ref[LANES:LANES + 1, :]
        denom = lane_at(denom_ref[...], h) + jnp.sum(phi * norm, 1, keepdims=True)
        rden = 1.0 / denom
        student = (numer_ref[h] + dot_wide(phi, state, 1, 1)) * rden
        err = student - teacher.astype(F32)
        loss_ref[...] += jnp.sum((err * err).reshape(count // EXTRA, EXTRA, LANES), 0)
        g = err * (2.0 / divisor)
        gn = g * rden
        gd = -jnp.sum(g * student, 1, keepdims=True) * rden
        back_ref[:LANES, :] += rows_wide(gn, phi)
        back_ref[LANES:, :] += only_row(jnp.sum(phi * gd, 0, keepdims=True), PAD)
        gn_more = jnp.concatenate([gn, first * gd], 1)
        linked = jnp.where(allowed, dot_exact_right(gn_more, v_more, 1, 1), 0.0)
        linked_t = jnp.where(turned, dot_exact_left(v_more, gn_more, 1, 1), 0.0)
        grad = dot_wide(linked, phik_ref[...], 1, 0) + dot_wide(gn, state, 1, 0) + gd * norm
        gpk_ref[...] += dot_wide(linked_t, phi, 1, 0)
        out_ref[h] = folded(rows_exact(q, feature_pull(phi, grad)))
    loss = jnp.sum(jnp.sum(loss_ref[...], 0, keepdims=True), 1, keepdims=True) * (1.0 / divisor)
    loss_ref[...] = jnp.broadcast_to(loss, (EXTRA, LANES))


def key_kernel(wanted, kv_ref, w_ref, phik_ref, gpk_ref, back_ref, twin_ref, gq_ref, *refs):
    parts = len(wanted)
    held, refs = refs[-parts:], refs[:-parts]
    flat_ref, pair_ref, sum_ref, sems = refs[-4:]
    far_refs = refs[:-4]
    counts = [want() for want in wanted]
    copies = [
        pltpu.make_async_copy(far, here, sems.at[at])
        for at, (far, here) in enumerate(zip(far_refs, held))
    ]
    for number, copy in zip(counts, copies):
        pl.when(number > 0)(copy.start)
    pair_ref[...] = back_ref[...] + twin_ref[...]

    def pulled(k, v, phi, of_ref, more, scale):
        grad = halves_added(dot(v, side_by_side(of_ref[:LANES, :]), 1, 0))
        grad = grad + of_ref[LANES:LANES + 1, :]
        return rows_exact(k, feature_pull(phi, more + scale * grad))

    scale = jnp.where(lax.axis_index("core") == 0, 1.0, 0.0)
    sum_ref[...] = pulled(
        kv_ref[:, :LANES], kv_ref[:, LANES:], phik_ref[...], twin_ref, gpk_ref[...], scale
    )
    for number, copy, here in zip(counts, copies, held):

        def visit(j, here=here):
            k = here[j, :, :LANES]
            phi = feature_map(k, signed(w_ref[0]))
            sum_ref[...] += pulled(k, here[j, :, LANES:], phi, pair_ref, 0.0, 1.0)

        pl.when(number > 0)(copy.wait)
        loop(number, visit)

    heads, half, _ = gq_ref.shape
    for h in range(heads):
        flat_ref[h * half:(h + 1) * half, :] = gq_ref[h]
    flat_ref[heads * half:, :] = folded(sum_ref[...])


def call(kernel, outs, *args, flops=0, exps=0, limit=16, scratch=(), away=0):
    shapes = [jax.ShapeDtypeStruct(shape, kind) for shape, kind in outs]
    moved = sum(math.prod(a.shape) * a.dtype.itemsize for a in list(args) + shapes)
    spaces = [pltpu.VMEM] * (len(args) - away) + [pl.ANY] * away
    return pl.pallas_call(
        kernel,
        out_shape=shapes,
        in_specs=[pl.BlockSpec(memory_space=space) for space in spaces],
        out_specs=[pl.BlockSpec(memory_space=pltpu.VMEM) for _ in shapes],
        scratch_shapes=list(scratch),
        compiler_params=pltpu.CompilerParams(vmem_limit_bytes=limit << 20),
        cost_estimate=pl.CostEstimate(flops=flops, bytes_accessed=moved, transcendentals=exps),
    )(*args)


def shift(x, axis, by):
    size = lax.axis_size(axis)
    return lax.ppermute(x, axis, [(i, (i + by) % size) for i in range(size)])


def shifts(x, axis):
    return [shift(x, axis, d) for d in range(1, lax.axis_size(axis))]


def swap(x, axis, bit):
    size = lax.axis_size(axis)
    return lax.ppermute(x, axis, [(i, (i ^ bit) % size) for i in range(size)])


def tree(pieces):
    if len(pieces) == 1:
        return pieces[0]
    return tree(pieces[0::2]) + tree(pieces[1::2])


def in_order(pieces, mine):
    count = len(pieces)
    return jnp.stack(
        [lax.select_n(lax.rem(mine - at + count, count), *pieces) for at in range(count)]
    )


def sum_ctx(x, y, core):
    pieces = x.reshape((NCORE, NY) + x.shape[1:])
    sent = lax.dynamic_index_in_dim(pieces, 1 - core, 0, False)
    part = lax.dynamic_index_in_dim(pieces, core, 0, False) + swap(sent, "core", 1)
    held = lax.dynamic_index_in_dim(part, y, 0, False)
    for d in range(1, NY):
        sent = lax.dynamic_index_in_dim(part, lax.rem(y + d, NY), 0, False)
        held = held + shift(sent, "y", d)
    held = held + swap(held, "z", 1)
    ahead, opposite, behind = (shift(held, "z", d) for d in (2, 4, 6))
    held = (held + opposite) + (ahead + behind)
    loss = held[-EXTRA, 0]
    held = held[:-EXTRA]
    mine = in_order([held] + shifts(held, "y"), y)
    other = swap(mine, "core", 1)
    both = [jnp.where(core == 0, mine, other), jnp.where(core == 0, other, mine)]
    return jnp.concatenate(both).reshape(-1, LANES), loss


def on_device(queries, keys, values, weight_q, weight_k):
    heads, head_dim, half = weight_q.shape
    rows = queries.shape[0]
    unit = math.log2(math.e) / math.sqrt(head_dim)
    z, y, core = (lax.axis_index(name) for name in ("z", "y", "core"))
    wq = jnp.swapaxes(weight_q, 1, 2)
    wk = jnp.swapaxes(weight_k, 1, 2)
    wide = ((heads, rows, head_dim), F32)
    both = ((2 * heads, rows, head_dim), F32)
    slim = ((rows, head_dim), F32)
    state_shape = ((head_dim + PAD, head_dim), F32)
    area = rows * rows * heads

    kv = jnp.concatenate([keys, values], -1)
    line = jnp.stack([kv] + shifts(kv, "y"))
    twin = swap(queries, "core", 1)
    twin_k = swap(keys, "core", 1)
    line, twin, twin_k = lax.optimization_barrier((line, twin, twin_k))

    def paired(bundle):
        return bundle.reshape(-1, 2 * rows, 2 * head_dim)

    qs, *carry, phi_k, state, numer, denom = call(
        functools.partial(near_kernel, heads, unit),
        [((2 * heads, rows, head_dim), BF16)] + [both] * 3 + [slim, state_shape, wide, slim],
        queries, twin, twin_k, kv, wq, wk, flops=area * head_dim * 18, exps=3 * area,
    )
    carry.append(jnp.zeros_like(state))

    def attend(carry, wanted, parts, last=False):
        keys_each = parts[0].shape[1]
        tokens = sum(part.shape[0] * keys_each for part in parts)
        packed = (((heads + 1) * rows + 2 * state.shape[0], head_dim), F32)
        more = [state] if last else []
        return call(
            functools.partial(far_kernel, heads, unit, wanted, last),
            [packed] * 2 if last else [both] * 3 + [state_shape],
            qs, wk, *carry, *parts, *more,
            flops=2 * rows * heads * tokens * head_dim * 4, exps=2 * rows * heads * tokens,
            scratch=[pltpu.VMEM(*kind) for kind in ([both] * 3 + [state_shape] if last else [])]
            + [pltpu.VMEM(parts[0].shape[1:], BF16)],
        )

    per = NY // 2

    def below(step, number=per):
        return lambda: jnp.where(lax.axis_index("z") >= step, number, 0)

    held = [line[1:]]
    wanted = [lambda: lax.axis_index("y")]
    carry = attend(carry, wanted, held)
    up, down = shift(line, "z", 1), shift(line, "z", -1)
    last = NZ // 2 - 1
    for step in range(1, last):
        carry, up, down = lax.optimization_barrier((carry, up, down))
        now = [paired(up), paired(down)]
        if step + 1 < last:
            up, down = shift(up, "z", 1), shift(down, "z", -1)
        else:
            passed = [shift(up[:per], "z", 1), shift(down[per:], "z", -1)]
            kept = [shift(up[per:], "z", 1), shift(down[:per], "z", -1)]
        held += now
        wanted += [below(step), below(NZ - step)]
        carry = attend(carry, wanted[-2:], now)
    carry, passed = lax.optimization_barrier((carry, passed))
    across = [shift(passed[0], "z", 1), shift(passed[1], "z", -1)]
    for now in (passed, kept):
        held += [paired(half) for half in now]
        wanted += [below(last, per // 2), below(NZ - last, per // 2)]
        carry = attend(carry, wanted[-2:], held[-2:])
    held.append(paired(jnp.concatenate(across)))
    wanted.append(below(NZ // 2))
    mine, pack = attend(carry, wanted[-1:], held[-1:], last=True)
    pack = swap(pack, "core", 1)

    places = NY * NCORE
    divisor = float(rows * NZ * places * heads * lax.axis_size("head"))
    teacher, back, loss, grown_q, gpk = call(
        functools.partial(grad_kernel, heads, divisor),
        [
            ((rows, heads * head_dim), BF16), state_shape, ((EXTRA, head_dim), F32),
            ((heads, half, head_dim), F32), slim,
        ],
        qs, kv, wq, phi_k, mine, pack, numer, denom,
        flops=area * head_dim * 30, scratch=[pltpu.VMEM(*state_shape)],
    )
    twin_back = swap(back, "core", 1)
    by_head = [loss] + shifts(loss, "head")
    q_rows = heads * half
    flat = (q_rows + half, head_dim)
    (grown,) = call(
        functools.partial(key_kernel, wanted),
        [(flat, F32)], kv, wk, phi_k, gpk, back, twin_back, grown_q, *held,
        flops=rows * head_dim * head_dim * 10 * NZ * NY, limit=52, away=len(held),
        scratch=[
            pltpu.VMEM(*state_shape), pltpu.VMEM((head_dim, head_dim), F32),
            pltpu.SemaphoreType.DMA((len(held),)),
        ] + [pltpu.VMEM(part.shape, BF16) for part in held],
    )
    grown, by_head = lax.optimization_barrier((grown, by_head))
    loss = tree(by_head)
    loss = jnp.broadcast_to(loss[None], (places,) + loss.shape)
    slices = grown.reshape(places, -1, head_dim)
    summed, loss = sum_ctx(jnp.concatenate([slices, loss], 1), y, core)
    grad_q = summed[:q_rows].reshape(heads, half, head_dim)
    grad_k = summed[q_rows:].reshape(1, half, head_dim)
    return (teacher, loss, jnp.swapaxes(grad_q, 1, 2), jnp.swapaxes(grad_k, 1, 2))


def solution(mesh):
    grid = Mesh(
        mesh.devices.reshape(NZ, NY, NCORE, mesh.devices.shape[1]), ("z", "y", "core", "head")
    )
    ctx = ("z", "y", "core")
    placed = (
        P(ctx, "head"),
        P(ctx, "head"),
        P(ctx, "head"),
        P("head", None, None),
        P("head", None, None),
    )
    return jax.shard_map(
        on_device,
        mesh=grid,
        in_specs=placed,
        out_specs=(P(ctx, "head"), P(), P("head", None, None), P("head", None, None)),
        check_vma=False,
    )
```

```python
import functools
import math

import jax
import jax.numpy as jnp
from jax import lax
from jax.experimental import pallas as pl
from jax.experimental.pallas import tpu as pltpu
from jax.sharding import Mesh, PartitionSpec as P

F32 = jnp.float32
BF16 = jnp.bfloat16
NEGATIVE = -1e30
TOO_LARGE = 2.0 ** 100
FINITE = 3.3e38
LANES = 128
EXTRA = 8
PAD = 16
NZ, NY, NCORE = 8, 4, 2


def dot(a, b, ca, cb):
    return lax.dot_general(a, b, (((ca,), (cb,)), ((), ())), preferred_element_type=F32)


def split(x):
    high = x.astype(BF16)
    return high, (x - high.astype(F32)).astype(BF16)


def dot_exact_right(x, e, cx, ce):
    high, low = split(x)
    return dot(high, e, cx, ce) + dot(low, e, cx, ce)


def dot_exact_left(e, x, ce, cx):
    high, low = split(x)
    return dot(e, high, ce, cx) + dot(e, low, ce, cx)


def dot_wide(x, y, cx, cy):
    xh, xl = split(x)
    yh, yl = split(y)
    return dot(xh, yh, cx, cy) + (dot(xh, yl, cx, cy) + dot(xl, yh, cx, cy))


def side_by_side(x):
    return jnp.concatenate(split(x), 1)


def halves_added(x):
    half = x.shape[1] // 2
    return x[:, :half] + x[:, half:]


def rows_exact(e, x):
    return halves_added(dot(e, side_by_side(x), 0, 0))


def rows_wide(x, y):
    both = halves_added(dot(side_by_side(x), side_by_side(y), 0, 0))
    half = both.shape[0] // 2
    return both[:half] + both[half:]


def lane_ids(shape):
    return lax.broadcasted_iota(jnp.int32, shape, 1)


def half_ones(depth):
    rows = lax.broadcasted_iota(jnp.int32, (depth, LANES), 0) & (LANES // 2)
    cols = lane_ids((depth, LANES)) & (LANES // 2)
    return jnp.where(rows == cols, 1.0, 0.0).astype(BF16)


def half_sums(high, low):
    return dot(jnp.concatenate([high, low], 1), half_ones(2 * LANES), 1, 0)


def feature_map(x, w2):
    e = jnp.exp(dot(x, w2, 1, 1))
    high = jnp.minimum(e, FINITE).astype(BF16)
    return e / half_sums(high, (e - high.astype(F32)).astype(BF16))


def signed(w):
    return jnp.concatenate([w, -w], 0)


def feature_pull(phi, grad):
    return phi * (grad - half_sums(*split(phi * grad)))


def row_total(x):
    return jnp.broadcast_to(jnp.sum(x, 1, keepdims=True), (x.shape[0], LANES))


def lane_wide(x, width):
    return jnp.concatenate([x] * (width // LANES), 1)


def lane_at(x, lane):
    return jnp.sum(jnp.where(lane_ids(x.shape) == lane, x, 0.0), 1, keepdims=True)


def lower_triangle(count):
    rows = lax.broadcasted_iota(jnp.int32, (count, count), 0)
    return lane_ids((count, count)) <= rows


def only_row(row, count):
    at = lax.broadcasted_iota(jnp.int32, (count, LANES), 0)
    return jnp.where(at == 0, row, 0.0)


def loop(count, body):
    def visit(index, unused):
        body(index)
        return unused

    lax.fori_loop(0, count, visit, 0)


def scores_of(q, k):
    return dot(q, jnp.concatenate([k, k], 1), 1, 1)


def add_state(k, v, phi, state_ref):
    state_ref[:LANES, :] += rows_exact(v, phi)
    state_ref[LANES:, :] += only_row(jnp.sum(phi, 0, keepdims=True), PAD)


def near_kernel(heads, unit, q_ref, twin_ref, twin_kv_ref, kv_ref, wq_ref, wk_ref, qs_ref,
                m_ref, l_ref, acc_ref, phik_ref, state_ref, numer_ref, denom_ref):
    count = kv_ref.shape[0]
    v = kv_ref[:, LANES:]
    state_ref[...] = jnp.zeros_like(state_ref)
    denom_ref[...] = jnp.zeros_like(denom_ref)
    k = kv_ref[:, :LANES]
    phi_k = feature_map(k, signed(wk_ref[0]))
    phik_ref[...] = phi_k
    add_state(k, v, phi_k, state_ref)
    for h in range(heads):
        cols = slice(h * LANES, (h + 1) * LANES)
        qs_ref[h] = side_by_side(q_ref[:, cols].astype(F32) * unit)
        qs_ref[heads + h] = side_by_side(twin_ref[:, cols].astype(F32) * unit)

    def head(h):
        allowed = lower_triangle(count)
        q = q_ref[:, pl.ds(pl.multiple_of(h * LANES, LANES), LANES)]
        s = jnp.where(allowed, scores_of(qs_ref[h], kv_ref[:, :LANES]), NEGATIVE)
        best = jnp.max(s, 1, keepdims=True)
        p = jnp.exp2(s - best)
        m_ref[h] = jnp.broadcast_to(best, (count, LANES))
        l_ref[h] = row_total(p)
        acc_ref[h] = dot(p.astype(BF16), v, 1, 0)
        s = jnp.where(allowed, scores_of(qs_ref[heads + h], twin_kv_ref[:, :LANES]), NEGATIVE)
        m_ref[heads + h] = jnp.broadcast_to(jnp.max(s, 1, keepdims=True), (count, LANES))
        l_ref[heads + h] = jnp.zeros((count, LANES), F32)
        acc_ref[heads + h] = jnp.zeros((count, LANES), F32)
        phi = feature_map(q, signed(wq_ref[h]))
        scores = jnp.where(allowed, dot_wide(phi, phik_ref[...], 1, 1), 0.0)
        numer_ref[h] = dot_exact_right(scores, v, 1, 0)
        denom_ref[...] = jnp.where(
            lane_ids((count, LANES)) == h, jnp.sum(scores, 1, keepdims=True), denom_ref[...]
        )

    loop(heads, head)

    def cross_head(h):
        s = scores_of(qs_ref[h], twin_kv_ref[:, :LANES])
        old = m_ref[h]
        new = jnp.maximum(old, jnp.max(s, 1, keepdims=True))
        fade = jnp.exp2(old - new)
        p = jnp.exp2(s - lane_wide(new, count))
        m_ref[h] = new
        l_ref[h] = l_ref[h] * fade + row_total(p)
        acc_ref[h] = acc_ref[h] * fade + dot(p.astype(BF16), twin_kv_ref[:, LANES:], 1, 0)

    loop(jnp.where(lax.axis_index("core") == 1, heads, 0), cross_head)


def far_kernel(heads, wanted, last, qs_ref, w_ref, mi_ref, li_ref, ai_ref, si_ref, *refs):
    parts = len(wanted)
    kv_refs, refs, chunk_ref = refs[:parts], refs[parts:-1], refs[-1]
    if last:
        near_ref, mine_ref, twin_ref, m_ref, l_ref, acc_ref, state_ref = refs
    else:
        m_ref, l_ref, acc_ref, state_ref = refs
    counts = [want() for want in wanted]
    tiles, count, _ = qs_ref.shape
    keys = kv_refs[0].shape[1]
    m_ref[...] = mi_ref[...]
    l_ref[...] = li_ref[...]
    acc_ref[...] = ai_ref[...]
    state_ref[...] = si_ref[...]

    def visit(index):
        ahead = 0
        for number, kv in zip(counts, kv_refs):

            @pl.when((index >= ahead) & (index < ahead + number))
            def _(kv=kv, ahead=ahead):
                chunk_ref[...] = kv[index - ahead]

            ahead = ahead + number
        k = chunk_ref[:, :LANES]
        twice = jnp.concatenate([k, k], 1)
        v = jnp.concatenate([chunk_ref[:, LANES:], jnp.ones((keys, LANES), BF16)], 1)
        following = dot(qs_ref[0], twice, 1, 1)
        for t in range(tiles):
            s = following
            if t + 1 < tiles:
                following = dot(qs_ref[t + 1], twice, 1, 1)
            p = jnp.exp2(s - lane_wide(m_ref[t], keys))
            grown = dot(p.astype(BF16), v, 1, 0)
            acc_ref[t] += grown[:, :LANES]
            l_ref[t] += grown[:, LANES:]
        add_state(k, chunk_ref[:, LANES:], feature_map(k, signed(w_ref[0])), state_ref)

    loop(sum(counts), visit)

    fine = jnp.max(l_ref[...]) < TOO_LARGE

    @pl.when(jnp.logical_not(fine))
    def _():
        m_ref[...] = mi_ref[...]
        l_ref[...] = li_ref[...]
        acc_ref[...] = ai_ref[...]
        for at in range(parts):
            kv = kv_refs[at]

            def again(index, kv=kv):
                j, t = index // tiles, lax.rem(index, tiles)
                s = scores_of(qs_ref[t], kv[j, :, :LANES])
                old = m_ref[t]
                new = jnp.maximum(old, jnp.max(s, 1, keepdims=True))
                fade = jnp.exp2(old - new)
                p = jnp.exp2(s - lane_wide(new, keys))
                m_ref[t] = new
                l_ref[t] = l_ref[t] * fade + row_total(p)
                acc_ref[t] = acc_ref[t] * fade + dot(p.astype(BF16), kv[j, :, LANES:], 1, 0)

            loop(counts[at] * tiles, again)

    if last:
        lanes = lane_ids((count, LANES))
        for first, out_ref in ((0, mine_ref), (heads, twin_ref)):
            stat = jnp.zeros((count, LANES), F32)
            for h in range(heads):
                t = first + h
                out_ref[h * count:(h + 1) * count, :] = acc_ref[t]
                stat = jnp.where(lanes == h, l_ref[t], stat)
                stat = jnp.where(lanes == heads + h, m_ref[t], stat)
            at = heads * count
            out_ref[at:at + count, :] = stat
            out_ref[at + count:at + count + LANES + PAD, :] = state_ref[...]
            out_ref[at + count + LANES + PAD:, :] = near_ref[...]


def folded(grown):
    half = LANES // 2
    turned = grown.T
    return turned[:half] - turned[half:]


def grad_kernel(heads, divisor, q_ref, kv_ref, w_ref, phik_ref, mine_ref, twin_ref, numer_ref,
                denom_ref, teacher_ref, back_ref, loss_ref, out_ref, gpk_ref, prev_ref):
    count = kv_ref.shape[0]
    at = heads * count
    stat, stat_twin = mine_ref[at:at + count, :], twin_ref[at:at + count, :]
    far, near = at + count, at + count + LANES + PAD
    later_core = jnp.where(lax.axis_index("core") == 1, 1.0, 0.0)
    prev_ref[...] = (
        mine_ref[far:near, :] + twin_ref[far:near, :] + later_core * twin_ref[near:, :]
    )
    back_ref[...] = jnp.zeros_like(back_ref)
    loss_ref[...] = jnp.zeros_like(loss_ref)
    gpk_ref[...] = jnp.zeros_like(gpk_ref)
    first = jnp.where(lane_ids((count, LANES)) == 0, 1.0, 0.0)
    v_more = jnp.concatenate([kv_ref[:, LANES:], first.astype(BF16)], 1)
    allowed = lower_triangle(count)
    turned = lax.broadcasted_iota(jnp.int32, (count, count), 0) <= lane_ids((count, count))
    for h in range(heads):
        m_mine = jnp.broadcast_to(lane_at(stat, heads + h), (count, LANES))
        m_twin = jnp.broadcast_to(lane_at(stat_twin, heads + h), (count, LANES))
        best = jnp.maximum(m_mine, m_twin)
        fade = jnp.exp2(m_mine - best)
        fade_twin = jnp.exp2(m_twin - best)
        total = lane_at(stat, h) * fade + lane_at(stat_twin, h) * fade_twin
        rows = slice(h * count, (h + 1) * count)
        teacher = ((mine_ref[rows, :] * fade + twin_ref[rows, :] * fade_twin) / total).astype(BF16)
        teacher_ref[:, h * LANES:(h + 1) * LANES] = teacher
        q = q_ref[:, h * LANES:(h + 1) * LANES]
        phi = feature_map(q, signed(w_ref[h]))
        state = prev_ref[:LANES, :]
        norm = prev_ref[LANES:LANES + 1, :]
        denom = lane_at(denom_ref[...], h) + jnp.sum(phi * norm, 1, keepdims=True)
        rden = 1.0 / denom
        student = (numer_ref[h] + dot_wide(phi, state, 1, 1)) * rden
        err = student - teacher.astype(F32)
        loss_ref[...] += jnp.sum((err * err).reshape(count // EXTRA, EXTRA, LANES), 0)
        g = err * (2.0 / divisor)
        gn = g * rden
        gd = -jnp.sum(g * student, 1, keepdims=True) * rden
        back_ref[:LANES, :] += rows_wide(gn, phi)
        back_ref[LANES:, :] += only_row(jnp.sum(phi * gd, 0, keepdims=True), PAD)
        gn_more = jnp.concatenate([gn, first * gd], 1)
        linked = jnp.where(allowed, dot_exact_right(gn_more, v_more, 1, 1), 0.0)
        linked_t = jnp.where(turned, dot_exact_left(v_more, gn_more, 1, 1), 0.0)
        grad = dot_wide(linked, phik_ref[...], 1, 0) + dot_wide(gn, state, 1, 0) + gd * norm
        gpk_ref[...] += dot_wide(linked_t, phi, 1, 0)
        out_ref[h] = folded(rows_exact(q, feature_pull(phi, grad)))
    loss = jnp.sum(jnp.sum(loss_ref[...], 0, keepdims=True), 1, keepdims=True) * (1.0 / divisor)
    loss_ref[...] = jnp.broadcast_to(loss, (EXTRA, LANES))


def key_kernel(wanted, kv_ref, w_ref, phik_ref, gpk_ref, back_ref, twin_ref, gq_ref, *refs):
    parts = len(wanted)
    held, refs = refs[-parts:], refs[:-parts]
    flat_ref, pair_ref, sum_ref, sems = refs[-4:]
    far_refs = refs[:-4]
    counts = [want() for want in wanted]
    copies = [
        pltpu.make_async_copy(far, here, sems.at[at])
        for at, (far, here) in enumerate(zip(far_refs, held))
    ]
    for number, copy in zip(counts, copies):
        pl.when(number > 0)(copy.start)
    pair_ref[...] = back_ref[...] + twin_ref[...]

    def pulled(k, v, phi, of_ref, more, scale):
        grad = halves_added(dot(v, side_by_side(of_ref[:LANES, :]), 1, 0))
        grad = grad + of_ref[LANES:LANES + 1, :]
        return rows_exact(k, feature_pull(phi, more + scale * grad))

    scale = jnp.where(lax.axis_index("core") == 0, 1.0, 0.0)
    sum_ref[...] = pulled(
        kv_ref[:, :LANES], kv_ref[:, LANES:], phik_ref[...], twin_ref, gpk_ref[...], scale
    )
    for number, copy, here in zip(counts, copies, held):

        def visit(j, here=here):
            k = here[j, :, :LANES]
            phi = feature_map(k, signed(w_ref[0]))
            sum_ref[...] += pulled(k, here[j, :, LANES:], phi, pair_ref, 0.0, 1.0)

        pl.when(number > 0)(copy.wait)
        loop(number, visit)

    heads, half, _ = gq_ref.shape
    for h in range(heads):
        flat_ref[h * half:(h + 1) * half, :] = gq_ref[h]
    flat_ref[heads * half:, :] = folded(sum_ref[...])


def call(kernel, outs, *args, flops=0, exps=0, limit=16, scratch=(), away=0):
    shapes = [jax.ShapeDtypeStruct(shape, kind) for shape, kind in outs]
    moved = sum(math.prod(a.shape) * a.dtype.itemsize for a in list(args) + shapes)
    spaces = [pltpu.VMEM] * (len(args) - away) + [pl.ANY] * away
    return pl.pallas_call(
        kernel,
        out_shape=shapes,
        in_specs=[pl.BlockSpec(memory_space=space) for space in spaces],
        out_specs=[pl.BlockSpec(memory_space=pltpu.VMEM) for _ in shapes],
        scratch_shapes=list(scratch),
        compiler_params=pltpu.CompilerParams(vmem_limit_bytes=limit << 20),
        cost_estimate=pl.CostEstimate(flops=flops, bytes_accessed=moved, transcendentals=exps),
    )(*args)


def shift(x, axis, by):
    size = lax.axis_size(axis)
    return lax.ppermute(x, axis, [(i, (i + by) % size) for i in range(size)])


def shifts(x, axis):
    return [shift(x, axis, d) for d in range(1, lax.axis_size(axis))]


def swap(x, axis, bit):
    size = lax.axis_size(axis)
    return lax.ppermute(x, axis, [(i, (i ^ bit) % size) for i in range(size)])


def tree(pieces):
    if len(pieces) == 1:
        return pieces[0]
    return tree(pieces[0::2]) + tree(pieces[1::2])


def in_order(pieces, mine):
    count = len(pieces)
    return jnp.stack(
        [lax.select_n(lax.rem(mine - at + count, count), *pieces) for at in range(count)]
    )


def sum_ctx(x, y, core):
    pieces = x.reshape((NCORE, NY) + x.shape[1:])
    sent = lax.dynamic_index_in_dim(pieces, 1 - core, 0, False)
    part = lax.dynamic_index_in_dim(pieces, core, 0, False) + swap(sent, "core", 1)
    held = lax.dynamic_index_in_dim(part, y, 0, False)
    for d in range(1, NY):
        sent = lax.dynamic_index_in_dim(part, lax.rem(y + d, NY), 0, False)
        held = held + shift(sent, "y", d)
    held = held + swap(held, "z", 1)
    ahead, opposite, behind = (shift(held, "z", d) for d in (2, 4, 6))
    held = (held + opposite) + (ahead + behind)
    loss = held[-EXTRA, 0]
    held = held[:-EXTRA]
    mine = in_order([held] + shifts(held, "y"), y)
    other = swap(mine, "core", 1)
    both = [jnp.where(core == 0, mine, other), jnp.where(core == 0, other, mine)]
    return jnp.concatenate(both).reshape(-1, LANES), loss


def on_device(queries, keys, values, weight_q, weight_k):
    heads, head_dim, half = weight_q.shape
    rows = queries.shape[0]
    unit = math.log2(math.e) / math.sqrt(head_dim)
    z, y, core = (lax.axis_index(name) for name in ("z", "y", "core"))
    wq = jnp.swapaxes(weight_q, 1, 2)
    wk = jnp.swapaxes(weight_k, 1, 2)
    wide = ((heads, rows, head_dim), F32)
    both = ((2 * heads, rows, head_dim), F32)
    slim = ((rows, head_dim), F32)
    state_shape = ((head_dim + PAD, head_dim), F32)
    area = rows * rows * heads

    kv = jnp.concatenate([keys, values], -1)
    line = jnp.stack([kv] + shifts(kv, "y"))
    twin = swap(queries, "core", 1)
    twin_kv = swap(kv, "core", 1)
    line, twin, twin_kv = lax.optimization_barrier((line, twin, twin_kv))

    def paired(bundle):
        return bundle.reshape(-1, 2 * rows, 2 * head_dim)

    qs, *carry, phi_k, state, numer, denom = call(
        functools.partial(near_kernel, heads, unit),
        [((2 * heads, rows, 2 * head_dim), BF16)] + [both] * 3 + [slim, state_shape, wide, slim],
        queries, twin, twin_kv, kv, wq, wk, flops=area * head_dim * 18, exps=3 * area,
    )
    carry.append(jnp.zeros_like(state))

    def attend(carry, wanted, parts, last=False):
        keys_each = parts[0].shape[1]
        tokens = sum(part.shape[0] * keys_each for part in parts)
        packed = (((heads + 1) * rows + 2 * state.shape[0], head_dim), F32)
        more = [state] if last else []
        return call(
            functools.partial(far_kernel, heads, wanted, last),
            [packed] * 2 if last else [both] * 3 + [state_shape],
            qs, wk, *carry, *parts, *more,
            flops=2 * rows * heads * tokens * head_dim * 4, exps=2 * rows * heads * tokens,
            scratch=[pltpu.VMEM(*kind) for kind in ([both] * 3 + [state_shape] if last else [])]
            + [pltpu.VMEM(parts[0].shape[1:], BF16)],
        )

    per = NY // 2

    def below(step, number=per):
        return lambda: jnp.where(lax.axis_index("z") >= step, number, 0)

    held = [line[1:]]
    wanted = [lambda: lax.axis_index("y")]
    carry = attend(carry, wanted, held)
    up, down = shift(line, "z", 1), shift(line, "z", -1)
    last = NZ // 2 - 1
    for step in range(1, last):
        carry, up, down = lax.optimization_barrier((carry, up, down))
        now = [paired(up), paired(down)]
        if step + 1 < last:
            up, down = shift(up, "z", 1), shift(down, "z", -1)
        else:
            passed = [shift(up[:per], "z", 1), shift(down[per:], "z", -1)]
            kept = [shift(up[per:], "z", 1), shift(down[:per], "z", -1)]
        held += now
        wanted += [below(step), below(NZ - step)]
        carry = attend(carry, wanted[-2:], now)
    carry, passed = lax.optimization_barrier((carry, passed))
    across = [shift(passed[0], "z", 1), shift(passed[1], "z", -1)]
    for now in (passed, kept):
        held += [paired(half) for half in now]
        wanted += [below(last, per // 2), below(NZ - last, per // 2)]
        carry = attend(carry, wanted[-2:], held[-2:])
    held.append(paired(jnp.concatenate(across)))
    wanted.append(below(NZ // 2))
    mine, pack = attend(carry, wanted[-1:], held[-1:], last=True)
    pack = swap(pack, "core", 1)

    places = NY * NCORE
    divisor = float(rows * NZ * places * heads * lax.axis_size("head"))
    teacher, back, loss, grown_q, gpk = call(
        functools.partial(grad_kernel, heads, divisor),
        [
            ((rows, heads * head_dim), BF16), state_shape, ((EXTRA, head_dim), F32),
            ((heads, half, head_dim), F32), slim,
        ],
        queries, kv, wq, phi_k, mine, pack, numer, denom,
        flops=area * head_dim * 30, scratch=[pltpu.VMEM(*state_shape)],
    )
    twin_back = swap(back, "core", 1)
    by_head = [loss] + shifts(loss, "head")
    q_rows = heads * half
    flat = (q_rows + half, head_dim)
    (grown,) = call(
        functools.partial(key_kernel, wanted),
        [(flat, F32)], kv, wk, phi_k, gpk, back, twin_back, grown_q, *held,
        flops=rows * head_dim * head_dim * 10 * NZ * NY, limit=52, away=len(held),
        scratch=[
            pltpu.VMEM(*state_shape), pltpu.VMEM((head_dim, head_dim), F32),
            pltpu.SemaphoreType.DMA((len(held),)),
        ] + [pltpu.VMEM(part.shape, BF16) for part in held],
    )
    grown, by_head = lax.optimization_barrier((grown, by_head))
    loss = tree(by_head)
    loss = jnp.broadcast_to(loss[None], (places,) + loss.shape)
    slices = grown.reshape(places, -1, head_dim)
    summed, loss = sum_ctx(jnp.concatenate([slices, loss], 1), y, core)
    grad_q = summed[:q_rows].reshape(heads, half, head_dim)
    grad_k = summed[q_rows:].reshape(1, half, head_dim)
    return (teacher, loss, jnp.swapaxes(grad_q, 1, 2), jnp.swapaxes(grad_k, 1, 2))


def solution(mesh):
    grid = Mesh(
        mesh.devices.reshape(NZ, NY, NCORE, mesh.devices.shape[1]), ("z", "y", "core", "head")
    )
    ctx = ("z", "y", "core")
    placed = (
        P(ctx, "head"),
        P(ctx, "head"),
        P(ctx, "head"),
        P("head", None, None),
        P("head", None, None),
    )
    return jax.shard_map(
        on_device,
        mesh=grid,
        in_specs=placed,
        out_specs=(P(ctx, "head"), P(), P("head", None, None), P("head", None, None)),
        check_vma=False,
    )
```

```python
import functools
import math

import jax
import jax.numpy as jnp
from jax import lax
from jax.experimental import pallas as pl
from jax.experimental.pallas import tpu as pltpu
from jax.sharding import Mesh, PartitionSpec as P

F32 = jnp.float32
BF16 = jnp.bfloat16
NEGATIVE = -1e30
TOO_LARGE = 2.0 ** 100
FINITE = 3.3e38
LANES = 128
EXTRA = 8
PAD = 16
NZ, NY, NCORE = 8, 4, 2


def dot(a, b, ca, cb):
    return lax.dot_general(a, b, (((ca,), (cb,)), ((), ())), preferred_element_type=F32)


def split(x):
    high = x.astype(BF16)
    return high, (x - high.astype(F32)).astype(BF16)


def dot_exact_right(x, e, cx, ce):
    high, low = split(x)
    return dot(high, e, cx, ce) + dot(low, e, cx, ce)


def dot_exact_left(e, x, ce, cx):
    high, low = split(x)
    return dot(e, high, ce, cx) + dot(e, low, ce, cx)


def dot_wide(x, y, cx, cy):
    xh, xl = split(x)
    yh, yl = split(y)
    return dot(xh, yh, cx, cy) + (dot(xh, yl, cx, cy) + dot(xl, yh, cx, cy))


def side_by_side(x):
    return jnp.concatenate(split(x), 1)


def halves_added(x):
    half = x.shape[1] // 2
    return x[:, :half] + x[:, half:]


def rows_exact(e, x):
    return halves_added(dot(e, side_by_side(x), 0, 0))


def rows_wide(x, y):
    both = halves_added(dot(side_by_side(x), side_by_side(y), 0, 0))
    half = both.shape[0] // 2
    return both[:half] + both[half:]


def lane_ids(shape):
    return lax.broadcasted_iota(jnp.int32, shape, 1)


def half_ones(depth):
    rows = lax.broadcasted_iota(jnp.int32, (depth, LANES), 0) & (LANES // 2)
    cols = lane_ids((depth, LANES)) & (LANES // 2)
    return jnp.where(rows == cols, 1.0, 0.0).astype(BF16)


def half_sums(high, low):
    return dot(jnp.concatenate([high, low], 1), half_ones(2 * LANES), 1, 0)


def feature_map(x, w2):
    e = jnp.exp(dot(x, w2, 1, 1))
    high = jnp.minimum(e, FINITE).astype(BF16)
    return e / half_sums(high, (e - high.astype(F32)).astype(BF16))


def signed(w):
    return jnp.concatenate([w, -w], 0)


def feature_pull(phi, grad):
    return phi * (grad - half_sums(*split(phi * grad)))


def row_total(x):
    return jnp.broadcast_to(jnp.sum(x, 1, keepdims=True), (x.shape[0], LANES))


def lane_wide(x, width):
    return jnp.concatenate([x] * (width // LANES), 1)


def lane_at(x, lane):
    return jnp.sum(jnp.where(lane_ids(x.shape) == lane, x, 0.0), 1, keepdims=True)


def lower_triangle(count):
    rows = lax.broadcasted_iota(jnp.int32, (count, count), 0)
    return lane_ids((count, count)) <= rows


def only_row(row, count):
    at = lax.broadcasted_iota(jnp.int32, (count, LANES), 0)
    return jnp.where(at == 0, row, 0.0)


def loop(count, body):
    def visit(index, unused):
        body(index)
        return unused

    lax.fori_loop(0, count, visit, 0)


def add_state(k, v, phi, state_ref):
    state_ref[:LANES, :] += rows_exact(v, phi)
    state_ref[LANES:, :] += only_row(jnp.sum(phi, 0, keepdims=True), PAD)


def near_kernel(heads, unit, q_ref, twin_ref, twin_k_ref, kv_ref, wq_ref, wk_ref, qs_ref,
                m_ref, l_ref, acc_ref, phik_ref, state_ref, numer_ref, denom_ref):
    count = kv_ref.shape[0]
    v = kv_ref[:, LANES:]
    state_ref[...] = jnp.zeros_like(state_ref)
    denom_ref[...] = jnp.zeros_like(denom_ref)
    k = kv_ref[:, :LANES]
    phi_k = feature_map(k, signed(wk_ref[0]))
    phik_ref[...] = phi_k
    add_state(k, v, phi_k, state_ref)
    for h in range(heads):
        qs_ref[h] = q_ref[:, h * LANES:(h + 1) * LANES]
        qs_ref[heads + h] = twin_ref[:, h * LANES:(h + 1) * LANES]

    def head(h):
        allowed = lower_triangle(count)
        q = qs_ref[h]
        s = jnp.where(allowed, dot(q, kv_ref[:, :LANES], 1, 1) * unit, NEGATIVE)
        best = jnp.max(s, 1, keepdims=True)
        p = jnp.exp2(s - best)
        m_ref[h] = jnp.broadcast_to(best, (count, LANES))
        l_ref[h] = row_total(p)
        acc_ref[h] = dot(p.astype(BF16), v, 1, 0)
        s = jnp.where(allowed, dot(qs_ref[heads + h], twin_k_ref[...], 1, 1) * unit, NEGATIVE)
        m_ref[heads + h] = jnp.broadcast_to(jnp.max(s, 1, keepdims=True), (count, LANES))
        l_ref[heads + h] = jnp.zeros((count, LANES), F32)
        acc_ref[heads + h] = jnp.zeros((count, LANES), F32)
        phi = feature_map(q, signed(wq_ref[h]))
        scores = jnp.where(allowed, dot_wide(phi, phik_ref[...], 1, 1), 0.0)
        numer_ref[h] = dot_exact_right(scores, v, 1, 0)
        denom_ref[...] = jnp.where(
            lane_ids((count, LANES)) == h, jnp.sum(scores, 1, keepdims=True), denom_ref[...]
        )

    loop(heads, head)

    def twin_head(h):
        at = heads + h
        s = dot(qs_ref[at], kv_ref[:, :LANES], 1, 1) * unit
        new = jnp.maximum(m_ref[at], jnp.max(s, 1, keepdims=True))
        p = jnp.exp2(s - lane_wide(new, count))
        m_ref[at] = new
        l_ref[at] = row_total(p)
        acc_ref[at] = dot(p.astype(BF16), v, 1, 0)

    loop(jnp.where(lax.axis_index("core") == 0, heads, 0), twin_head)


def far_kernel(heads, unit, wanted, last, qs_ref, w_ref, mi_ref, li_ref, ai_ref, si_ref, *refs):
    parts = len(wanted)
    kv_refs, refs, chunk_ref = refs[:parts], refs[parts:-1], refs[-1]
    if last:
        near_ref, mine_ref, twin_ref, m_ref, l_ref, acc_ref, state_ref = refs
    else:
        m_ref, l_ref, acc_ref, state_ref = refs
    counts = [want() for want in wanted]
    tiles, count, _ = qs_ref.shape
    keys = kv_refs[0].shape[1]
    m_ref[...] = mi_ref[...]
    l_ref[...] = li_ref[...]
    acc_ref[...] = ai_ref[...]
    state_ref[...] = si_ref[...]

    def visit(index):
        ahead = 0
        for number, kv in zip(counts, kv_refs):

            @pl.when((index >= ahead) & (index < ahead + number))
            def _(kv=kv, ahead=ahead):
                chunk_ref[...] = kv[index - ahead]

            ahead = ahead + number
        k = chunk_ref[:, :LANES]
        v = jnp.concatenate([chunk_ref[:, LANES:], jnp.ones((keys, LANES), BF16)], 1)
        following = dot(qs_ref[0], k, 1, 1)
        for t in range(tiles):
            s = following
            if t + 1 < tiles:
                following = dot(qs_ref[t + 1], k, 1, 1)
            p = jnp.exp2(s * unit - lane_wide(m_ref[t], keys))
            grown = dot(p.astype(BF16), v, 1, 0)
            acc_ref[t] += grown[:, :LANES]
            l_ref[t] += grown[:, LANES:]
        add_state(k, chunk_ref[:, LANES:], feature_map(k, signed(w_ref[0])), state_ref)

    loop(sum(counts), visit)

    fine = jnp.max(l_ref[...]) < TOO_LARGE

    @pl.when(jnp.logical_not(fine))
    def _():
        m_ref[...] = mi_ref[...]
        l_ref[...] = li_ref[...]
        acc_ref[...] = ai_ref[...]
        for at in range(parts):
            kv = kv_refs[at]

            def again(index, kv=kv):
                j, t = index // tiles, lax.rem(index, tiles)
                s = dot(qs_ref[t], kv[j, :, :LANES], 1, 1) * unit
                old = m_ref[t]
                new = jnp.maximum(old, jnp.max(s, 1, keepdims=True))
                fade = jnp.exp2(old - new)
                p = jnp.exp2(s - lane_wide(new, keys))
                m_ref[t] = new
                l_ref[t] = l_ref[t] * fade + row_total(p)
                acc_ref[t] = acc_ref[t] * fade + dot(p.astype(BF16), kv[j, :, LANES:], 1, 0)

            loop(counts[at] * tiles, again)

    if last:
        lanes = lane_ids((count, LANES))
        for first, out_ref in ((0, mine_ref), (heads, twin_ref)):
            stat = jnp.zeros((count, LANES), F32)
            for h in range(heads):
                t = first + h
                out_ref[h * count:(h + 1) * count, :] = acc_ref[t]
                stat = jnp.where(lanes == h, l_ref[t], stat)
                stat = jnp.where(lanes == heads + h, m_ref[t], stat)
            at = heads * count
            out_ref[at:at + count, :] = stat
            out_ref[at + count:at + count + LANES + PAD, :] = state_ref[...]
            out_ref[at + count + LANES + PAD:, :] = near_ref[...]


def folded(grown):
    half = LANES // 2
    turned = grown.T
    return turned[:half] - turned[half:]


def grad_kernel(heads, divisor, qs_ref, kv_ref, w_ref, phik_ref, mine_ref, twin_ref, numer_ref,
                denom_ref, teacher_ref, back_ref, loss_ref, out_ref, gpk_ref, prev_ref):
    count = kv_ref.shape[0]
    at = heads * count
    stat, stat_twin = mine_ref[at:at + count, :], twin_ref[at:at + count, :]
    far, near = at + count, at + count + LANES + PAD
    later_core = jnp.where(lax.axis_index("core") == 1, 1.0, 0.0)
    prev_ref[...] = (
        mine_ref[far:near, :] + twin_ref[far:near, :] + later_core * twin_ref[near:, :]
    )
    back_ref[...] = jnp.zeros_like(back_ref)
    loss_ref[...] = jnp.zeros_like(loss_ref)
    gpk_ref[...] = jnp.zeros_like(gpk_ref)
    first = jnp.where(lane_ids((count, LANES)) == 0, 1.0, 0.0)
    v_more = jnp.concatenate([kv_ref[:, LANES:], first.astype(BF16)], 1)
    allowed = lower_triangle(count)
    turned = lax.broadcasted_iota(jnp.int32, (count, count), 0) <= lane_ids((count, count))
    for h in range(heads):
        m_mine = jnp.broadcast_to(lane_at(stat, heads + h), (count, LANES))
        m_twin = jnp.broadcast_to(lane_at(stat_twin, heads + h), (count, LANES))
        best = jnp.maximum(m_mine, m_twin)
        fade = jnp.exp2(m_mine - best)
        fade_twin = jnp.exp2(m_twin - best)
        total = lane_at(stat, h) * fade + lane_at(stat_twin, h) * fade_twin
        rows = slice(h * count, (h + 1) * count)
        teacher = ((mine_ref[rows, :] * fade + twin_ref[rows, :] * fade_twin) / total).astype(BF16)
        teacher_ref[:, h * LANES:(h + 1) * LANES] = teacher
        q = qs_ref[h]
        phi = feature_map(q, signed(w_ref[h]))
        state = prev_ref[:LANES, :]
        norm = prev_ref[LANES:LANES + 1, :]
        denom = lane_at(denom_ref[...], h) + jnp.sum(phi * norm, 1, keepdims=True)
        rden = 1.0 / denom
        student = (numer_ref[h] + dot_wide(phi, state, 1, 1)) * rden
        err = student - teacher.astype(F32)
        loss_ref[...] += jnp.sum((err * err).reshape(count // EXTRA, EXTRA, LANES), 0)
        g = err * (2.0 / divisor)
        gn = g * rden
        gd = -jnp.sum(g * student, 1, keepdims=True) * rden
        back_ref[:LANES, :] += rows_wide(gn, phi)
        back_ref[LANES:, :] += only_row(jnp.sum(phi * gd, 0, keepdims=True), PAD)
        gn_more = jnp.concatenate([gn, first * gd], 1)
        linked = jnp.where(allowed, dot_exact_right(gn_more, v_more, 1, 1), 0.0)
        linked_t = jnp.where(turned, dot_exact_left(v_more, gn_more, 1, 1), 0.0)
        grad = dot_wide(linked, phik_ref[...], 1, 0) + dot_wide(gn, state, 1, 0) + gd * norm
        gpk_ref[...] += dot_wide(linked_t, phi, 1, 0)
        out_ref[h] = folded(rows_exact(q, feature_pull(phi, grad)))
    loss = jnp.sum(jnp.sum(loss_ref[...], 0, keepdims=True), 1, keepdims=True) * (1.0 / divisor)
    loss_ref[...] = jnp.broadcast_to(loss, (EXTRA, LANES))


def key_kernel(wanted, kv_ref, w_ref, phik_ref, gpk_ref, back_ref, twin_ref, gq_ref, *refs):
    parts = len(wanted)
    held, refs = refs[-parts:], refs[:-parts]
    flat_ref, pair_ref, sum_ref, sems = refs[-4:]
    far_refs = refs[:-4]
    counts = [want() for want in wanted]
    copies = [
        pltpu.make_async_copy(far, here, sems.at[at])
        for at, (far, here) in enumerate(zip(far_refs, held))
    ]
    for number, copy in zip(counts, copies):
        pl.when(number > 0)(copy.start)
    pair_ref[...] = back_ref[...] + twin_ref[...]

    def pulled(k, v, phi, of_ref, more, scale):
        grad = halves_added(dot(v, side_by_side(of_ref[:LANES, :]), 1, 0))
        grad = grad + of_ref[LANES:LANES + 1, :]
        return rows_exact(k, feature_pull(phi, more + scale * grad))

    scale = jnp.where(lax.axis_index("core") == 0, 1.0, 0.0)
    sum_ref[...] = pulled(
        kv_ref[:, :LANES], kv_ref[:, LANES:], phik_ref[...], twin_ref, gpk_ref[...], scale
    )
    for number, copy, here in zip(counts, copies, held):

        def visit(j, here=here):
            k = here[j, :, :LANES]
            phi = feature_map(k, signed(w_ref[0]))
            sum_ref[...] += pulled(k, here[j, :, LANES:], phi, pair_ref, 0.0, 1.0)

        pl.when(number > 0)(copy.wait)
        loop(number, visit)

    heads, half, _ = gq_ref.shape
    for h in range(heads):
        flat_ref[h * half:(h + 1) * half, :] = gq_ref[h]
    flat_ref[heads * half:, :] = folded(sum_ref[...])


def call(kernel, outs, *args, flops=0, exps=0, limit=16, scratch=(), away=0):
    shapes = [jax.ShapeDtypeStruct(shape, kind) for shape, kind in outs]
    moved = sum(math.prod(a.shape) * a.dtype.itemsize for a in list(args) + shapes)
    spaces = [pltpu.VMEM] * (len(args) - away) + [pl.ANY] * away
    return pl.pallas_call(
        kernel,
        out_shape=shapes,
        in_specs=[pl.BlockSpec(memory_space=space) for space in spaces],
        out_specs=[pl.BlockSpec(memory_space=pltpu.VMEM) for _ in shapes],
        scratch_shapes=list(scratch),
        compiler_params=pltpu.CompilerParams(vmem_limit_bytes=limit << 20),
        cost_estimate=pl.CostEstimate(flops=flops, bytes_accessed=moved, transcendentals=exps),
    )(*args)


def shift(x, axis, by):
    size = lax.axis_size(axis)
    return lax.ppermute(x, axis, [(i, (i + by) % size) for i in range(size)])


def shifts(x, axis):
    return [shift(x, axis, d) for d in range(1, lax.axis_size(axis))]


def swap(x, axis, bit):
    size = lax.axis_size(axis)
    return lax.ppermute(x, axis, [(i, (i ^ bit) % size) for i in range(size)])


def tree(pieces):
    if len(pieces) == 1:
        return pieces[0]
    return tree(pieces[0::2]) + tree(pieces[1::2])


def in_order(pieces, mine):
    count = len(pieces)
    return jnp.stack(
        [lax.select_n(lax.rem(mine - at + count, count), *pieces) for at in range(count)]
    )


def sum_ctx(x, y, core):
    held = jnp.sum(lax.all_to_all(x, ("y", "core"), 0, 0), 0)
    copies = jnp.broadcast_to(held[None], (NZ,) + held.shape)
    held = jnp.sum(lax.all_to_all(copies, "z", 0, 0), 0)
    loss = held[-EXTRA, 0]
    held = held[:-EXTRA]
    mine = in_order([held] + shifts(held, "y"), y)
    other = swap(mine, "core", 1)
    both = [jnp.where(core == 0, mine, other), jnp.where(core == 0, other, mine)]
    return jnp.stack(both, 1).reshape(-1, LANES), loss


def on_device(queries, keys, values, weight_q, weight_k):
    heads, head_dim, half = weight_q.shape
    rows = queries.shape[0]
    unit = math.log2(math.e) / math.sqrt(head_dim)
    z, y, core = (lax.axis_index(name) for name in ("z", "y", "core"))
    wq = jnp.swapaxes(weight_q, 1, 2)
    wk = jnp.swapaxes(weight_k, 1, 2)
    wide = ((heads, rows, head_dim), F32)
    both = ((2 * heads, rows, head_dim), F32)
    slim = ((rows, head_dim), F32)
    state_shape = ((head_dim + PAD, head_dim), F32)
    area = rows * rows * heads

    kv = jnp.concatenate([keys, values], -1)
    line = jnp.stack([kv] + shifts(kv, "y"))
    twin = swap(queries, "core", 1)
    twin_k = swap(keys, "core", 1)
    line, twin, twin_k = lax.optimization_barrier((line, twin, twin_k))

    def paired(bundle):
        return bundle.reshape(-1, 2 * rows, 2 * head_dim)

    qs, *carry, phi_k, state, numer, denom = call(
        functools.partial(near_kernel, heads, unit),
        [((2 * heads, rows, head_dim), BF16)] + [both] * 3 + [slim, state_shape, wide, slim],
        queries, twin, twin_k, kv, wq, wk, flops=area * head_dim * 18, exps=3 * area,
    )
    carry.append(jnp.zeros_like(state))

    def attend(carry, wanted, parts, last=False):
        keys_each = parts[0].shape[1]
        tokens = sum(part.shape[0] * keys_each for part in parts)
        packed = (((heads + 1) * rows + 2 * state.shape[0], head_dim), F32)
        more = [state] if last else []
        return call(
            functools.partial(far_kernel, heads, unit, wanted, last),
            [packed] * 2 if last else [both] * 3 + [state_shape],
            qs, wk, *carry, *parts, *more,
            flops=2 * rows * heads * tokens * head_dim * 4, exps=2 * rows * heads * tokens,
            scratch=[pltpu.VMEM(*kind) for kind in ([both] * 3 + [state_shape] if last else [])]
            + [pltpu.VMEM(parts[0].shape[1:], BF16)],
        )

    per = NY // 2

    def below(step, number=per):
        return lambda: jnp.where(lax.axis_index("z") >= step, number, 0)

    held = [line[1:]]
    wanted = [lambda: lax.axis_index("y")]
    carry = attend(carry, wanted, held)
    up, down = shift(line, "z", 1), shift(line, "z", -1)
    last = NZ // 2 - 1
    for step in range(1, last):
        carry, up, down = lax.optimization_barrier((carry, up, down))
        now = [paired(up), paired(down)]
        if step + 1 < last:
            up, down = shift(up, "z", 1), shift(down, "z", -1)
        else:
            passed = [shift(up[:per], "z", 1), shift(down[per:], "z", -1)]
            kept = [shift(up[per:], "z", 1), shift(down[:per], "z", -1)]
        held += now
        wanted += [below(step), below(NZ - step)]
        carry = attend(carry, wanted[-2:], now)
    carry, passed = lax.optimization_barrier((carry, passed))
    across = [shift(passed[0], "z", 1), shift(passed[1], "z", -1)]
    for now in (passed, kept):
        held += [paired(half) for half in now]
        wanted += [below(last, per // 2), below(NZ - last, per // 2)]
        carry = attend(carry, wanted[-2:], held[-2:])
    held.append(paired(jnp.concatenate(across)))
    wanted.append(below(NZ // 2))
    mine, pack = attend(carry, wanted[-1:], held[-1:], last=True)
    pack = swap(pack, "core", 1)

    places = NY * NCORE
    divisor = float(rows * NZ * places * heads * lax.axis_size("head"))
    teacher, back, loss, grown_q, gpk = call(
        functools.partial(grad_kernel, heads, divisor),
        [
            ((rows, heads * head_dim), BF16), state_shape, ((EXTRA, head_dim), F32),
            ((heads, half, head_dim), F32), slim,
        ],
        qs, kv, wq, phi_k, mine, pack, numer, denom,
        flops=area * head_dim * 30, scratch=[pltpu.VMEM(*state_shape)],
    )
    twin_back = swap(back, "core", 1)
    by_head = [loss] + shifts(loss, "head")
    q_rows = heads * half
    flat = (q_rows + half, head_dim)
    (grown,) = call(
        functools.partial(key_kernel, wanted),
        [(flat, F32)], kv, wk, phi_k, gpk, back, twin_back, grown_q, *held,
        flops=rows * head_dim * head_dim * 10 * NZ * NY, limit=52, away=len(held),
        scratch=[
            pltpu.VMEM(*state_shape), pltpu.VMEM((head_dim, head_dim), F32),
            pltpu.SemaphoreType.DMA((len(held),)),
        ] + [pltpu.VMEM(part.shape, BF16) for part in held],
    )
    grown, by_head = lax.optimization_barrier((grown, by_head))
    loss = tree(by_head)
    loss = jnp.broadcast_to(loss[None], (places,) + loss.shape)
    slices = grown.reshape(places, -1, head_dim)
    summed, loss = sum_ctx(jnp.concatenate([slices, loss], 1), y, core)
    grad_q = summed[:q_rows].reshape(heads, half, head_dim)
    grad_k = summed[q_rows:].reshape(1, half, head_dim)
    return (teacher, loss, jnp.swapaxes(grad_q, 1, 2), jnp.swapaxes(grad_k, 1, 2))


def solution(mesh):
    grid = Mesh(
        mesh.devices.reshape(NZ, NY, NCORE, mesh.devices.shape[1]), ("z", "y", "core", "head")
    )
    ctx = ("z", "y", "core")
    placed = (
        P(ctx, "head"),
        P(ctx, "head"),
        P(ctx, "head"),
        P("head", None, None),
        P("head", None, None),
    )
    return jax.shard_map(
        on_device,
        mesh=grid,
        in_specs=placed,
        out_specs=(P(ctx, "head"), P(), P("head", None, None), P("head", None, None)),
        check_vma=False,
    )
```
